32 devices in a mesh: narrow: 4 (over y, x), wide: 8 (over z, core).
Axes of the slice: x: 2, y: 2, z: 4, core: 2. Of those that a mesh axis runs over, the one named last changes fastest.
Arguments:
- tokens: bfloat16 [4096, 2, 1024], P(('wide', 'narrow')), may hold values from -6 to 6
- gain_attn: float32 [1024], replicated, may hold values from 0.5 to 1.5
- w_query: bfloat16 [1024, 1024], P(None, 'narrow'), may hold values from -0.109375 to 0.109375
- w_key: bfloat16 [1024, 512], P(None, 'narrow'), may hold values from -0.109375 to 0.109375
- w_value: bfloat16 [1024, 512], P(None, 'narrow'), may hold values from -0.1875 to 0.1875
- w_out: bfloat16 [1024, 1024], P('narrow'), may hold values from -0.375 to 0.375
- gain_moe: float32 [1024], replicated, may hold values from 0.5 to 1.5
- w_router: bfloat16 [1024, 16], replicated, may hold values from -0.08984375 to 0.08984375
- w_gate: bfloat16 [16, 1024, 512], P('wide'), may hold values from -0.1875 to 0.1875
- w_up: bfloat16 [16, 1024, 512], P('wide'), may hold values from -0.1875 to 0.1875
- w_down: bfloat16 [16, 512, 1024], P('wide'), may hold values from -0.75 to 0.75
- routes: int32 [4096, 2, 8], P(('wide', 'narrow')), may hold values from 0 to 15, all different within a row; in each aligned block of 256 rows (0 to 255, 256 to 511, ..., all dimensions but the last counted through in order) at most 192 rows name the same one
- rope_scale: float32 [1], replicated, may hold values from 1 to 4
- cotangent: bfloat16 [4096, 2, 1024], P(('wide', 'narrow')), may hold values from -6 to 6
Outputs:
- mixed: bfloat16 [4096, 2, 1024], P(('wide', 'narrow'))
- grad_tokens: float32 [4096, 2, 1024], P(('wide', 'narrow'))
- grad_gain_attn: float32 [1024], replicated
- grad_w_query: float32 [1024, 1024], P('wide', 'narrow')
- grad_w_key: float32 [1024, 512], P('wide', 'narrow')
- grad_w_value: float32 [1024, 512], P('wide', 'narrow')
- grad_w_out: float32 [1024, 1024], P('narrow', 'wide')
- grad_gain_moe: float32 [1024], replicated
- grad_router: float32 [1024, 16], replicated
- grad_gate: float32 [16, 1024, 512], P('wide', 'narrow')
- grad_up: float32 [16, 1024, 512], P('wide', 'narrow')
- grad_down: float32 [16, 512, 1024], P('wide', 'narrow')
The draws below stay inside these ranges and needn't reach their ends.
Inputs may be any that keep to these rules, and one draw needn't show every extreme that they name: `routes`: each token names 8 different experts. Among the tokens of one device no expert is named more than 192 times, a bound that some block reaches.
All inputs are finite; a program needn't handle non-finite values.
Results may differ from the reference program's by a relative error of at most 0.028.
Values may be sent and summed in bfloat16 or wider, within the bound.
A program may use at most 192 MiB of HBM per device.

```python
import math
import jax
import jax.numpy as jnp
import numpy as np
from jax import lax

D = 1024
FF = 512
H = 16
KVH = 8
HD = 64
TOP = 8
SEQS = 2
EXPERTS = 16
SEQ = 4096
TOK_DEV = 256
CAP = 192


def block_levels(own_key, shape, cuts, low, high):
    loudness = 1.0
    for axis_at, blocks in cuts:
        steps = jax.random.uniform(jax.random.fold_in(jax.random.fold_in(own_key, 6), axis_at), (blocks,), jnp.float32, low / len(cuts), high / len(cuts))
        loudness = loudness * jnp.repeat(jnp.exp(steps), shape[axis_at] // blocks).reshape((-1,) + (1,) * (len(shape) - 1 - axis_at))
    return loudness


def shared_out(own_key, own, number, rows, count, top, reach, slope):
    sequence = jax.random.permutation(own_key, count)
    heavy_load, ordinary = portions_of(count, rows * top, reach, slope, True), portions_of(count, rows * top, reach, slope, False)
    places = jnp.arange(count)

    def named(lengths, offset_by):
        used = int((lengths > 0).sum())
        fixed = max(1, used // 4)
        moved = fixed + (places - fixed + offset_by * (used - fixed)) % max(1, count - fixed)
        return jnp.zeros((count,), jnp.int32).at[sequence[jnp.where(places < fixed, places, moved)]].set(jnp.asarray(lengths, jnp.int32))

    lengths = jnp.where(number % 4 == 0, named(heavy_load, number // 4), named(ordinary, number - number // 4 - 1))
    mixed = jax.random.permutation(jax.random.fold_in(own, 3), count)
    donor, sink = mixed[0:count // 2 * 2:2], mixed[1:count // 2 * 2:2]
    slack = jnp.minimum(lengths[donor] - 1, reach - lengths[sink]) // 2
    slack = jnp.where((donor == sequence[0]) | (sink == sequence[0]) | (lengths[sink] == 0), 0, jnp.maximum(slack, 0))
    moved = jax.random.randint(jax.random.fold_in(own, 4), (count // 2,), 0, 1 << 20) % (slack + 1)
    lengths = lengths.at[donor].add(-moved).at[sink].add(moved)
    members = jnp.searchsorted(jnp.cumsum(lengths), jnp.arange(rows * top), side="right").astype(jnp.int32)
    table = members.reshape(top, rows).T
    table = table[jax.random.permutation(jax.random.fold_in(own, 1), rows)]
    offset_by = jax.random.randint(jax.random.fold_in(own, 2), (rows, 1), 0, top)
    return jnp.take_along_axis(table, (jnp.arange(top)[None, :] + offset_by) % top, axis=1)


def portions_of(count, total, reach, slope, full):
    loads = [(1 << 20) // math.isqrt(rank ** slope) + 1 for rank in range(1, count + 1)]
    largest = reach if full else min(reach, max(-(-total // count), total * loads[0] // sum(loads)))
    least = 1 if total - largest >= count - 1 else 0
    holding, spare = [largest] + [least] * (count - 1), total - largest - least * (count - 1)
    while spare > 0:
        free = [i for i in range(1, count) if holding[i] < largest] or [i for i in range(1, count) if holding[i] < reach]
        whole, left = sum([loads[i] for i in free]), spare
        for i in free:
            more = min(reach - holding[i], max(1, left * loads[i] // whole), spare)
            holding[i] = holding[i] + more
            spare = spare - more
    return np.array(holding)


def scatter_about(stream_key, dims, spread, reach, split=(), kind=jnp.bfloat16):
    values = spread * jax.random.normal(stream_key, dims, jnp.float32)
    if split:
        values = values * block_levels(stream_key, dims, split, -0.22, 0.18)
    return jnp.clip(values, -reach, reach).astype(kind)


def setup_inputs(seed: int = 0) -> dict:
    streams_of = jax.random.split(jax.random.key(seed), 15)
    tokens = scatter_about(streams_of[0], (SEQ, SEQS, D), 1.0, 6.0, ((0, 32),))
    gain_attn = jnp.clip(1.0 + 0.1 * jax.random.normal(streams_of[1], (D,), jnp.float32), 0.5, 1.5)
    w_query = scatter_about(streams_of[2], (D, H * HD), (3 * D) ** -0.5, 0.109375, ((1, 4),))
    w_key = scatter_about(streams_of[3], (D, KVH * HD), (3 * D) ** -0.5, 0.109375, ((1, 4),))
    w_value = scatter_about(streams_of[4], (D, KVH * HD), D ** -0.5, 0.1875, ((1, 4),))
    w_out = scatter_about(streams_of[5], (H * HD, D), (H * HD // 4) ** -0.5, 0.375, ((0, 4),))
    gain_moe = jnp.clip(1.0 + 0.1 * jax.random.normal(streams_of[6], (D,), jnp.float32), 0.5, 1.5)
    w_router = scatter_about(streams_of[7], (D, EXPERTS), 0.015625, 0.08984375)
    w_gate = scatter_about(streams_of[8], (EXPERTS, D, FF), D ** -0.5, 0.1875, ((0, 8),))
    w_up = scatter_about(streams_of[9], (EXPERTS, D, FF), D ** -0.5, 0.1875, ((0, 8),))
    w_down = scatter_about(streams_of[10], (EXPERTS, FF, D), (FF // 8) ** -0.5, 0.75, ((0, 8),))
    routes_keys = jax.random.split(jax.random.fold_in(streams_of[11], 1), SEQ * SEQS // TOK_DEV)
    routes_turns = jax.random.permutation(jax.random.fold_in(streams_of[11], 3), SEQ * SEQS // TOK_DEV)
    routes = jax.vmap(lambda own, number: shared_out(jax.random.fold_in(streams_of[11], 2), own, number, TOK_DEV, EXPERTS, TOP, CAP, 1))(routes_keys, routes_turns).reshape((SEQ, SEQS, TOP))
    rope_scale = jnp.clip(jax.random.uniform(streams_of[12], (1,), jnp.float32, 1.0, 4.0), 1.0, 4.0)
    cotangent = scatter_about(streams_of[13], (SEQ, SEQS, D), 1.0, 6.0, ((0, 32),))
    return dict(tokens=tokens, gain_attn=gain_attn, w_query=w_query, w_key=w_key, w_value=w_value, w_out=w_out, gain_moe=gain_moe, w_router=w_router, w_gate=w_gate, w_up=w_up, w_down=w_down, routes=routes, rope_scale=rope_scale, cotangent=cotangent)


EPSILON = 1e-06
ROPE_BASE = 10000.0
MASKED = -1e+30
PRECISE = lax.Precision.HIGHEST

@jax.custom_vjp
def low(v):
    return lax.optimization_barrier(v.astype(jnp.bfloat16)).astype(jnp.float32)

@jax.custom_vjp
def low_back(v):
    return v

def low_keep(v):
    return (low(v), None)

def low_pass(kept, grad):
    return (grad,)

def back_keep(v):
    return (v, None)

def back_low(kept, grad):
    return (low(grad),)
low.defvjp(low_keep, low_pass)
low_back.defvjp(back_keep, back_low)

def normalize(inputs, gain_vector):
    return inputs * lax.rsqrt(lax.optimization_barrier(jnp.mean(inputs * inputs, axis=-1, keepdims=True)) + EPSILON) * gain_vector

def rotate(tensor, positions, factor, direction):
    half_size = tensor.shape[-1] // 2
    frequency = ROPE_BASE ** (-jnp.arange(half_size, dtype=jnp.float32) * 2.0 / tensor.shape[-1])
    angles = (positions.astype(jnp.float32) / factor)[:, None] * frequency[None, :]
    cosine = jnp.cos(angles)[:, None, None, :]
    sine_part = direction * jnp.sin(angles)[:, None, None, :]
    leading = tensor[..., :half_size]
    trailing = tensor[..., half_size:]
    return jnp.concatenate([leading * cosine - trailing * sine_part, trailing * cosine + leading * sine_part], axis=-1)

def project(matrix_left, matrix_right):
    return jnp.einsum('tsd,dc->tsc', matrix_left, matrix_right, precision=PRECISE)

def attention(queries, key_heads, value_heads):
    block_size = math.gcd(SEQ, 512)
    block_count = SEQ // block_size
    query_blocks = queries.reshape(block_count, block_size, SEQS, KVH, H // KVH, HD)
    key_pos = jnp.arange(SEQ)

    def one_block(pieces):
        query_part, block_start = pieces
        query_pos = block_start + jnp.arange(block_size)
        scores = jnp.einsum('qskgd,tskd->skgqt', query_part, key_heads, precision=PRECISE) * HD ** (-0.5)
        scores = jnp.where(key_pos[None, :] <= query_pos[:, None], scores, MASKED)
        scores = low_back(scores)
        weights = low(jax.nn.softmax(scores, axis=-1))
        return jnp.einsum('skgqt,tskd->qskgd', weights, value_heads, precision=PRECISE)
    outputs = lax.map(jax.checkpoint(one_block), (query_blocks, jnp.arange(block_count) * block_size))
    return outputs.reshape(SEQ, SEQS, H * HD)

def reference(tokens, gain_attn, w_query, w_key, w_value, w_out, gain_moe, w_router, w_gate, w_up, w_down, routes, rope_scale, cotangent):
    positions = jnp.arange(SEQ)
    factor = rope_scale[0]
    expert_ids = routes.reshape(SEQ * SEQS, TOP)
    onehot = (expert_ids[:, :, None] == jnp.arange(EXPERTS).astype(jnp.int32)[None, None, :]).astype(jnp.float32)

    def forward(token_float, gain_one, query_weight, key_weight, value_weight, out_weight, gain_two, router_weight, gate_weight, up_weight, down_weight):
        attn_low = low(normalize(token_float, gain_one))
        query_pre = low_back(project(attn_low, query_weight)).reshape(SEQ, SEQS, H, HD)
        queries = low(rotate(query_pre, positions, factor, 1.0)).reshape(SEQ, SEQS, KVH, H // KVH, HD)
        key_pre = low_back(project(attn_low, key_weight)).reshape(SEQ, SEQS, KVH, HD)
        key_heads = low(rotate(key_pre, positions, factor, 1.0))
        value_heads = low_back(low(project(attn_low, value_weight))).reshape(SEQ, SEQS, KVH, HD)
        attended = low_back(low(attention(queries, key_heads, value_heads)))
        branch = low_back(project(attended, out_weight))
        residual = token_float + branch
        moe_low = low(normalize(residual, gain_two)).reshape(SEQ * SEQS, D)
        logits = jnp.dot(moe_low, router_weight, precision=PRECISE)
        chosen = lax.optimization_barrier(jnp.sum(onehot * logits[:, None, :], axis=-1))
        gate_weights = jax.nn.softmax(chosen, axis=-1)
        shares = lax.optimization_barrier(jnp.sum(gate_weights[:, :, None] * onehot, axis=1))

        def expert_step(running, pieces):
            expert_gate, expert_up, expert_down, expert_share = pieces
            inputs = low_back(moe_low)
            gate_part = low_back(jnp.dot(inputs, expert_gate, precision=PRECISE))
            up_part = low_back(jnp.dot(inputs, expert_up, precision=PRECISE))
            hidden = low(jax.nn.silu(gate_part) * up_part)
            result = low_back(low(jnp.dot(hidden, expert_down, precision=PRECISE)))
            return (running + expert_share[:, None] * result, None)
        moe_sum, unused = lax.scan(jax.checkpoint(expert_step), jnp.zeros((SEQ * SEQS, D), jnp.float32), (gate_weight, up_weight, down_weight, shares.T))
        return residual + moe_sum.reshape(SEQ, SEQS, D)
    primals = (tokens.astype(jnp.float32), gain_attn, w_query.astype(jnp.float32), w_key.astype(jnp.float32), w_value.astype(jnp.float32), w_out.astype(jnp.float32), gain_moe, w_router.astype(jnp.float32), w_gate.astype(jnp.float32), w_up.astype(jnp.float32), w_down.astype(jnp.float32))
    output, pullback = jax.vjp(forward, *primals)
    gradients = pullback(cotangent.astype(jnp.float32))
    return (output.astype(jnp.bfloat16), gradients[0], gradients[1], gradients[2], gradients[3], gradients[4], gradients[5], gradients[6], gradients[7], gradients[8], gradients[9], gradients[10])
```

```python
import jax
import jax.numpy as jnp
from jax import lax
from jax.sharding import PartitionSpec as P

HD = 64


EPSILON = 1e-06
ROPE_BASE = 10000.0
MASKED = -1e30
PRECISE = lax.Precision.HIGHEST


def rotate(tensor, positions, factor, direction):
    half_size = tensor.shape[-1] // 2
    frequency = ROPE_BASE ** (-jnp.arange(half_size, dtype=jnp.float32) * 2.0 / tensor.shape[-1])
    angles = (positions.astype(jnp.float32) / factor)[:, None] * frequency[None, :]
    cosine = jnp.cos(angles)[:, None, None, :]
    sine_part = direction * jnp.sin(angles)[:, None, None, :]
    leading = tensor[..., :half_size]
    trailing = tensor[..., half_size:]
    return jnp.concatenate(
        [leading * cosine - trailing * sine_part, trailing * cosine + leading * sine_part], axis=-1
    )


def normalize(inputs, gain_vector):
    inverse = lax.rsqrt(jnp.mean(inputs * inputs, axis=-1, keepdims=True) + EPSILON)
    return (inputs * inverse * gain_vector, inverse)


def normalize_back(inputs, inverse, gain_vector, upstream):
    scaled = inputs * inverse
    through = upstream * gain_vector
    input_grad = inverse * (through - scaled * jnp.mean(through * scaled, axis=-1, keepdims=True))
    gain_grad = jnp.sum(upstream * scaled, axis=(0, 1))
    return (input_grad, gain_grad)


def block_scores(query_group, key_block, query_pos, key_pos, score_scale):
    products = (
        jnp.einsum("qskgd,tskd->skgqt", query_group, key_block, preferred_element_type=jnp.float32)
        * score_scale
    )
    return jnp.where(key_pos[None, :] <= query_pos[:, None], products, MASKED)


def block_backward(
    query_group,
    attended_group,
    log_total,
    row_inner,
    key_block,
    value_block,
    query_pos,
    key_pos,
    score_scale,
):
    scores = block_scores(query_group, key_block, query_pos, key_pos, score_scale)
    attention = jnp.exp(scores - log_total[..., None])
    prob_grads = jnp.einsum(
        "qskgd,tskd->skgqt", attended_group, value_block, preferred_element_type=jnp.float32
    )
    score_grads = (attention * (prob_grads - row_inner[..., None])).astype(jnp.bfloat16)
    query_grad = score_scale * jnp.einsum(
        "skgqt,tskd->qskgd", score_grads, key_block, preferred_element_type=jnp.float32
    )
    key_grad = score_scale * jnp.einsum(
        "skgqt,qskgd->tskd", score_grads, query_group, preferred_element_type=jnp.float32
    )
    value_grad = jnp.einsum(
        "skgqt,qskgd->tskd",
        attention.astype(jnp.bfloat16),
        attended_group,
        preferred_element_type=jnp.float32,
    )
    return (query_grad, key_grad, value_grad)


def on_device(
    tokens,
    gain_attn,
    w_query,
    w_key,
    w_value,
    w_out,
    gain_moe,
    w_router,
    w_gate,
    w_up,
    w_down,
    routes,
    rope_scale,
    cotangent,
):
    narrow_count = lax.axis_size("narrow")
    wide_count = lax.axis_size("wide")
    wide_place = lax.axis_index("wide")
    local_rows, sequences, model_width = tokens.shape
    block_rows = local_rows * narrow_count
    head_size = HD
    query_cols = w_query.shape[1]
    kv_cols = w_key.shape[1]
    kv_heads = kv_cols // head_size
    group_size = query_cols // kv_cols
    score_scale = head_size ** (-0.5)
    factor = rope_scale[0]
    token_float = tokens.astype(jnp.float32)
    attn_normed, attn_inverse = normalize(token_float, gain_attn)
    attn_low = attn_normed.astype(jnp.bfloat16)
    attn_block = lax.all_gather(attn_low, "narrow", axis=0, tiled=True)
    joint_weight = jnp.concatenate([w_query, w_key, w_value], axis=1)
    joint_proj = jnp.einsum(
        "tsd,dc->tsc", attn_block, joint_weight, preferred_element_type=jnp.float32
    )
    query_pos = wide_place * block_rows + lax.iota(jnp.int32, block_rows)
    query_rot = rotate(
        joint_proj[..., :query_cols].reshape(
            block_rows, sequences, kv_heads * group_size, head_size
        ),
        query_pos,
        factor,
        1.0,
    )
    query_group = query_rot.astype(jnp.bfloat16).reshape(
        block_rows, sequences, kv_heads, group_size, head_size
    )
    key_rot = rotate(
        joint_proj[..., query_cols : query_cols + kv_cols].reshape(
            block_rows, sequences, kv_heads, head_size
        ),
        query_pos,
        factor,
        1.0,
    )
    key_local = key_rot.astype(jnp.bfloat16).reshape(block_rows, sequences, kv_cols)
    value_local = joint_proj[..., query_cols + kv_cols :].astype(jnp.bfloat16)
    pair_local = jnp.concatenate([key_local, value_local], axis=-1)
    pair_all = lax.all_gather(pair_local, "wide", axis=0, tiled=True)

    def split_pair(block_index):
        pair_block = lax.dynamic_slice_in_dim(pair_all, block_index * block_rows, block_rows, 0)
        key_block = pair_block[..., :kv_cols].reshape(block_rows, sequences, kv_heads, head_size)
        value_block = pair_block[..., kv_cols:].reshape(block_rows, sequences, kv_heads, head_size)
        key_pos = block_index * block_rows + lax.iota(jnp.int32, block_rows)
        return (key_block, value_block, key_pos)

    def forward_block(block_index, carried):
        running, denominator, accumulated = carried
        key_block, value_block, key_pos = split_pair(block_index)
        scores = block_scores(query_group, key_block, query_pos, key_pos, score_scale)
        new_running = jnp.maximum(running, jnp.max(scores, axis=-1))
        rescale = jnp.exp(running - new_running)
        weights = jnp.exp(scores - new_running[..., None])
        denominator = denominator * rescale + jnp.sum(weights, axis=-1)
        accumulated = accumulated * rescale[..., None] + jnp.einsum(
            "skgqt,tskd->skgqd",
            weights.astype(jnp.bfloat16),
            value_block,
            preferred_element_type=jnp.float32,
        )
        return (new_running, denominator, accumulated)

    stat_shape = (sequences, kv_heads, group_size, block_rows)
    starting = (
        jnp.full(stat_shape, MASKED, jnp.float32),
        jnp.zeros(stat_shape, jnp.float32),
        jnp.zeros(stat_shape + (head_size,), jnp.float32),
    )
    running, denominator, accumulated = lax.fori_loop(0, wide_place + 1, forward_block, starting)
    attn_result = accumulated / denominator[..., None]
    log_total = running + jnp.log(denominator)
    out_tokens = attn_result.transpose(3, 0, 1, 2, 4).reshape(block_rows, sequences, query_cols)
    out_low = out_tokens.astype(jnp.bfloat16)
    rows_part = out_low
    attn_branch = lax.psum_scatter(
        jnp.einsum("tsc,cd->tsd", rows_part, w_out, preferred_element_type=jnp.float32).astype(
            jnp.bfloat16
        ),
        "narrow",
        scatter_dimension=0,
        tiled=True,
    ).astype(jnp.float32)
    residual = token_float + attn_branch
    moe_normed, moe_inverse = normalize(residual, gain_moe)
    moe_low = moe_normed.astype(jnp.bfloat16)
    token_count = local_rows * sequences
    moe_flat = moe_low.reshape(token_count, model_width)
    expert_count = w_router.shape[1]
    local_experts = w_gate.shape[0]
    choose = routes.shape[-1]
    expert_ids = routes.reshape(token_count, choose)
    onehot = (expert_ids[:, :, None] == lax.iota(jnp.int32, expert_count)[None, None, :]).astype(
        jnp.float32
    )
    named = jnp.sum(onehot, axis=1)
    logits = jnp.dot(moe_flat, w_router, preferred_element_type=jnp.float32)
    masked = jnp.where(named > 0, logits, MASKED)
    powers = jnp.exp(masked - jnp.max(masked, axis=-1, keepdims=True)) * named
    shares = powers / jnp.sum(powers, axis=-1, keepdims=True)
    upstream = cotangent.astype(jnp.float32)
    upstream_flat = upstream.reshape(token_count, model_width)
    upstream_all = lax.all_gather(
        cotangent.reshape(token_count, model_width), "wide", axis=0, tiled=True
    )
    moe_all = lax.all_gather(moe_flat, "wide", axis=0, tiled=True)
    shares_all = lax.all_gather(shares, "wide", axis=0, tiled=True)
    first_expert = wide_place * local_experts
    own_shares = lax.dynamic_slice_in_dim(shares_all, first_expert, local_experts, 1).T
    gate_part = jnp.einsum("td,edf->etf", moe_all, w_gate, preferred_element_type=jnp.float32)
    up_part = jnp.einsum("td,edf->etf", moe_all, w_up, preferred_element_type=jnp.float32)
    down_back = jnp.einsum("td,efd->etf", upstream_all, w_down, preferred_element_type=jnp.float32)
    sigmoid_gate = jax.nn.sigmoid(gate_part)
    activated = gate_part * sigmoid_gate
    hidden = activated * up_part
    hidden_low = hidden.astype(jnp.bfloat16)
    own_picks = jnp.sum(hidden * down_back, axis=-1)
    hidden_shared = (hidden * own_shares[:, :, None]).astype(jnp.bfloat16)
    part_out = jnp.einsum("etf,efd->td", hidden_shared, w_down, preferred_element_type=jnp.float32)
    hidden_grads = down_back * own_shares[:, :, None]
    slope = sigmoid_gate * (1.0 + gate_part * (1.0 - sigmoid_gate))
    gate_signal = (hidden_grads * up_part * slope).astype(jnp.bfloat16)
    up_signal = (hidden_grads * activated).astype(jnp.bfloat16)
    input_grads = jnp.einsum(
        "etf,edf->td", gate_signal, w_gate, preferred_element_type=jnp.float32
    ) + jnp.einsum("etf,edf->td", up_signal, w_up, preferred_element_type=jnp.float32)
    pick_high = own_picks.T.astype(jnp.bfloat16)
    pick_low = (own_picks.T - pick_high.astype(jnp.float32)).astype(jnp.bfloat16)
    pick_pair = jnp.zeros((moe_all.shape[0], 2, expert_count), jnp.bfloat16)
    pick_pair = lax.dynamic_update_slice(
        pick_pair, jnp.stack([pick_high, pick_low], axis=1), (0, 0, first_expert)
    ).reshape(moe_all.shape[0], 2 * expert_count)
    pick_pair = lax.psum_scatter(pick_pair, "wide", scatter_dimension=0, tiled=True).astype(
        jnp.float32
    )
    moe_part = lax.psum_scatter(
        part_out.astype(jnp.bfloat16), "wide", scatter_dimension=0, tiled=True
    ).astype(jnp.float32)
    copy_sum = lax.psum_scatter(
        input_grads.astype(jnp.bfloat16), "wide", scatter_dimension=0, tiled=True
    ).astype(jnp.float32)
    layer_out = (residual + moe_part.reshape(local_rows, sequences, model_width)).astype(
        jnp.bfloat16
    )
    picks = pick_pair[:, :expert_count] + pick_pair[:, expert_count:]
    logit_grads = shares * (picks - jnp.sum(shares * picks, axis=-1, keepdims=True))
    router_grads = jnp.dot(moe_flat.astype(jnp.float32).T, logit_grads, precision=PRECISE)
    moe_grads = jnp.dot(logit_grads, w_router.astype(jnp.float32).T, precision=PRECISE)
    moe_grads = moe_grads + copy_sum
    down_update = jnp.einsum(
        "etf,td->efd", hidden_shared, upstream_all, preferred_element_type=jnp.float32
    )
    gate_update = jnp.einsum("td,etf->edf", moe_all, gate_signal, preferred_element_type=jnp.float32)
    up_update = jnp.einsum("td,etf->edf", moe_all, up_signal, preferred_element_type=jnp.float32)
    expert_grads = (
        lax.psum_scatter(
            gate_update.astype(jnp.bfloat16), "narrow", scatter_dimension=1, tiled=True
        ).astype(jnp.float32),
        lax.psum_scatter(
            up_update.astype(jnp.bfloat16), "narrow", scatter_dimension=1, tiled=True
        ).astype(jnp.float32),
        lax.psum_scatter(
            down_update.astype(jnp.bfloat16), "narrow", scatter_dimension=1, tiled=True
        ).astype(jnp.float32),
    )
    norm_grads, moe_gain = normalize_back(
        residual, moe_inverse, gain_moe, moe_grads.reshape(local_rows, sequences, model_width)
    )
    residual_grads = upstream + norm_grads
    branch_low = residual_grads.astype(jnp.bfloat16)
    branch_all = lax.all_gather(branch_low, "narrow", axis=0, tiled=True)
    out_update = jnp.einsum("tsc,tsd->cd", out_low, branch_all, preferred_element_type=jnp.float32)
    attended_grads = jnp.einsum(
        "tsd,cd->tsc", branch_all, w_out, preferred_element_type=jnp.float32
    ).astype(jnp.bfloat16)
    attended_group = attended_grads.reshape(block_rows, sequences, kv_heads, group_size, head_size)
    row_inner = jnp.sum(
        attended_group.astype(jnp.float32).transpose(1, 2, 3, 0, 4) * attn_result, axis=-1
    )
    query_zero = jnp.zeros((block_rows, sequences, kv_heads, group_size, head_size), jnp.float32)

    def both_block(block_index, carried):
        query_grads, pair_grads = carried
        key_block, value_block, key_pos = split_pair(block_index)
        query_part, key_grad, value_grad = block_backward(
            query_group,
            attended_group,
            log_total,
            row_inner,
            key_block,
            value_block,
            query_pos,
            key_pos,
            score_scale,
        )
        pair_part = jnp.concatenate(
            [
                key_grad.reshape(block_rows, sequences, kv_cols),
                value_grad.reshape(block_rows, sequences, kv_cols),
            ],
            axis=-1,
        )
        pair_grads = lax.dynamic_update_slice_in_dim(
            pair_grads, pair_part, block_index * block_rows, 0
        )
        return (query_grads + query_part, pair_grads)

    pair_zero = jnp.zeros((block_rows * wide_count, sequences, 2 * kv_cols), jnp.float32)
    query_grads, pair_grads = lax.fori_loop(0, wide_place + 1, both_block, (query_zero, pair_zero))
    pair_own = lax.psum_scatter(
        pair_grads.astype(jnp.bfloat16), "wide", scatter_dimension=0, tiled=True
    ).astype(jnp.float32)
    query_low = (
        rotate(
            query_grads.reshape(block_rows, sequences, kv_heads * group_size, head_size),
            query_pos,
            factor,
            -1.0,
        )
        .astype(jnp.bfloat16)
        .reshape(block_rows, sequences, query_cols)
    )
    key_low = (
        rotate(
            pair_own[..., :kv_cols].reshape(block_rows, sequences, kv_heads, head_size),
            query_pos,
            factor,
            -1.0,
        )
        .astype(jnp.bfloat16)
        .reshape(block_rows, sequences, kv_cols)
    )
    value_low = pair_own[..., kv_cols:].astype(jnp.bfloat16)
    joint_grads = jnp.concatenate([query_low, key_low, value_low], axis=-1)
    joint_update = jnp.einsum(
        "tsd,tsc->dc", attn_block, joint_grads, preferred_element_type=jnp.float32
    )
    rows_part = joint_grads
    attn_grads = lax.psum_scatter(
        jnp.einsum(
            "tsc,dc->tsd", rows_part, joint_weight, preferred_element_type=jnp.float32
        ).astype(jnp.bfloat16),
        "narrow",
        scatter_dimension=0,
        tiled=True,
    ).astype(jnp.float32)
    token_grads, attn_gain = normalize_back(token_float, attn_inverse, gain_attn, attn_grads)
    token_grads = residual_grads + token_grads
    joint_summed, out_summed = (
        lax.psum_scatter(
            joint_update.astype(jnp.bfloat16), "wide", scatter_dimension=0, tiled=True
        ).astype(jnp.float32),
        lax.psum_scatter(
            out_update.T.astype(jnp.bfloat16), "wide", scatter_dimension=0, tiled=True
        ).astype(jnp.float32),
    )
    moe_small = lax.psum(
        jnp.concatenate([moe_gain[:, None], router_grads], axis=1), ("narrow", "wide")
    )
    summed_small = (
        lax.psum(attn_gain, ("narrow", "wide")),
        moe_small[:, 0],
        moe_small[:, 1:],
    )
    return (
        layer_out,
        token_grads,
        summed_small[0],
        joint_summed[:, :query_cols],
        joint_summed[:, query_cols : query_cols + kv_cols],
        joint_summed[:, query_cols + kv_cols :],
        out_summed.T,
        summed_small[1],
        summed_small[2],
        expert_grads[0],
        expert_grads[1],
        expert_grads[2],
    )


def solution(mesh):
    return jax.shard_map(
        on_device,
        mesh=mesh,
        in_specs=(
            P(("wide", "narrow"), None, None),
            P(),
            P(None, "narrow"),
            P(None, "narrow"),
            P(None, "narrow"),
            P("narrow", None),
            P(),
            P(),
            P("wide", None, None),
            P("wide", None, None),
            P("wide", None, None),
            P(("wide", "narrow"), None, None),
            P(),
            P(("wide", "narrow"), None, None),
        ),
        out_specs=(
            P(("wide", "narrow"), None, None),
            P(("wide", "narrow"), None, None),
            P(),
            P("wide", "narrow"),
            P("wide", "narrow"),
            P("wide", "narrow"),
            P("narrow", "wide"),
            P(),
            P(),
            P("wide", "narrow", None),
            P("wide", "narrow", None),
            P("wide", "narrow", None),
        ),
        check_vma=False,
    )
```

```python
import functools

import jax
import jax.numpy as jnp
from jax import lax
from jax.experimental import pallas as pl
from jax.experimental.pallas import tpu as pltpu
from jax.sharding import PartitionSpec as P

HD = 64


EPSILON = 1e-06
ROPE_BASE = 10000.0
MASKED = -1e30
PRECISE = lax.Precision.HIGHEST
VMEM_BYTES = 56 << 20


def dot_t(left, right):
    return lax.dot_general(left, right, (((1,), (1,)), ((), ())), preferred_element_type=jnp.float32)


def dot_n(left, right):
    return lax.dot_general(left, right, (((1,), (0,)), ((), ())), preferred_element_type=jnp.float32)


def dot_c(left, right):
    return lax.dot_general(left, right, (((0,), (0,)), ((), ())), preferred_element_type=jnp.float32)


def head_mask(shape, head):
    lane = lax.broadcasted_iota(jnp.int32, shape, len(shape) - 1)
    return jnp.logical_and(lane >= head * HD, lane < (head + 1) * HD)


def only_head(block, head):
    if block.shape[-1] == HD:
        return block
    return jnp.where(head_mask(block.shape, head), block, jnp.zeros_like(block))


def attn_fwd_kernel(place_ref, q_ref, k_ref, v_ref, o_ref, low_ref, log_ref, top_ref, sum_ref, acc_ref):
    step = pl.program_id(1)
    place = place_ref[0]
    groups, rows, cols = q_ref.shape[1:]
    pairs = [(group, head) for group in range(groups) for head in range(cols // HD)]

    @pl.when(step == 0)
    def _():
        top_ref[...] = jnp.full(top_ref.shape, MASKED, jnp.float32)
        sum_ref[...] = jnp.zeros(sum_ref.shape, jnp.float32)
        acc_ref[...] = jnp.zeros(acc_ref.shape, jnp.float32)

    def one(masked):
        key_block = k_ref[0]

        def scores_of(number):
            group, head = pairs[number]
            return dot_t(key_block, only_head(q_ref[0, group], head))

        ahead = scores_of(0)
        for number, (group, head) in enumerate(pairs):
            part = pl.ds(number * rows, rows)
            lanes = pl.ds(head * HD, HD)
            scores = ahead
            if number + 1 < len(pairs):
                ahead = scores_of(number + 1)
            if masked:
                row = lax.broadcasted_iota(jnp.int32, scores.shape, 0)
                col = lax.broadcasted_iota(jnp.int32, scores.shape, 1)
                scores = jnp.where(row <= col, scores, MASKED)
            old = top_ref[:1, part]
            new = jnp.maximum(old, jnp.max(scores, axis=0, keepdims=True))
            fade = jnp.exp(old - new)
            weights = jnp.exp(scores - new)
            sum_ref[:1, part] = sum_ref[:1, part] * fade + jnp.sum(weights, axis=0, keepdims=True)
            acc_ref[group, lanes, :] = acc_ref[group, lanes, :] * fade + dot_n(
                v_ref[0, lanes, :], weights.astype(jnp.bfloat16)
            )
            top_ref[:1, part] = new

    @pl.when(step < place)
    def _():
        one(False)

    @pl.when(step == place)
    def _():
        one(True)
        for number, (group, head) in enumerate(pairs):
            part = pl.ds(number * rows, rows)
            lanes = pl.ds(head * HD, HD)
            total = sum_ref[:1, part]
            acc_ref[group, lanes, :] = acc_ref[group, lanes, :] / total
            log_ref[0, :, part] = jnp.broadcast_to(top_ref[:1, part] + jnp.log(total), (8, rows))
        for group in range(groups):
            result = jnp.transpose(acc_ref[group])
            o_ref[0, group] = result
            low_ref[0, group] = result.astype(jnp.bfloat16)


def attn_fwd(place, q, k, v_turned):
    seqs, groups, rows, cols = q.shape
    count = k.shape[1] // rows
    heads = groups * cols // HD
    whole = pl.BlockSpec((1, groups, rows, cols), lambda s, j, p: (s, 0, 0, 0))
    return pl.pallas_call(
        attn_fwd_kernel,
        grid_spec=pltpu.PrefetchScalarGridSpec(
            num_scalar_prefetch=1,
            grid=(seqs, count),
            in_specs=[
                whole,
                pl.BlockSpec((1, rows, cols), lambda s, j, p: (s, jnp.minimum(j, p[0]), 0)),
                pl.BlockSpec((1, cols, rows), lambda s, j, p: (s, 0, jnp.minimum(j, p[0]))),
            ],
            out_specs=[whole, whole, pl.BlockSpec((1, 8, heads * rows), lambda s, j, p: (s, 0, 0))],
            scratch_shapes=[
                pltpu.VMEM((8, heads * rows), jnp.float32),
                pltpu.VMEM((8, heads * rows), jnp.float32),
                pltpu.VMEM((groups, cols, rows), jnp.float32),
            ],
        ),
        out_shape=[
            jax.ShapeDtypeStruct(q.shape, jnp.float32),
            jax.ShapeDtypeStruct(q.shape, jnp.bfloat16),
            jax.ShapeDtypeStruct((seqs, 8, heads * rows), jnp.float32),
        ],
        compiler_params=pltpu.CompilerParams(vmem_limit_bytes=VMEM_BYTES),
        name="attention_forward",
    )(place, q, k, v_turned)


def attn_bwd_kernel(scale, place_ref, q_ref, g_ref, o_ref, log_ref, k_ref, v_ref, dq_ref, dk_ref, dv_ref, inner_ref, acc_ref):
    step = pl.program_id(1)
    place = place_ref[0]
    groups, rows, cols = q_ref.shape[1:]
    pairs = [(group, head) for group in range(groups) for head in range(cols // HD)]

    @pl.when(step == 0)
    def _():
        acc_ref[...] = jnp.zeros(acc_ref.shape, jnp.float32)
        ones = jnp.ones((8, cols), jnp.float32)
        for number, (group, head) in enumerate(pairs):
            prod = only_head(g_ref[0, group].astype(jnp.float32) * o_ref[0, group], head)
            inner_ref[:, pl.ds(number * rows, rows)] = lax.dot_general(
                ones, prod, (((1,), (1,)), ((), ())), precision=PRECISE, preferred_element_type=jnp.float32
            )

    def one(masked):
        key_block = k_ref[0]
        value_block = v_ref[0]
        dk = jnp.zeros(dk_ref.shape[1:], jnp.float32)
        dv = jnp.zeros(dv_ref.shape[1:], jnp.float32)

        def ahead_of(number):
            group, head = pairs[number]
            q = only_head(q_ref[0, group], head)
            g = only_head(g_ref[0, group], head)
            return q, g, dot_t(key_block, q), dot_t(value_block, g)

        ahead = ahead_of(0)
        for number, (group, head) in enumerate(pairs):
            part = pl.ds(number * rows, rows)
            q, g, scores, back = ahead
            if number + 1 < len(pairs):
                ahead = ahead_of(number + 1)
            probs = jnp.exp(scores - log_ref[0, :1, part])
            if masked:
                row = lax.broadcasted_iota(jnp.int32, scores.shape, 0)
                col = lax.broadcasted_iota(jnp.int32, scores.shape, 1)
                probs = jnp.where(row <= col, probs, 0.0)
            grads = (probs * (back - inner_ref[:1, part])).astype(jnp.bfloat16)
            dv = dv + dot_n(probs.astype(jnp.bfloat16), g)
            dk = dk + dot_n(grads, q)
            acc_ref[group] = acc_ref[group] + dot_c(grads, only_head(key_block, head))
        dk_ref[0] = dk.astype(dk_ref.dtype)
        dv_ref[0] = dv.astype(dv_ref.dtype)

    @pl.when(step < place)
    def _():
        one(False)

    @pl.when(step == place)
    def _():
        one(True)
        dq_ref[0] = acc_ref[...] * scale

    @pl.when(step > place)
    def _():
        dk_ref[...] = jnp.zeros(dk_ref.shape, dk_ref.dtype)
        dv_ref[...] = jnp.zeros(dv_ref.shape, dv_ref.dtype)


def attn_bwd(scale, place, q, g, o, logs, k, v):
    seqs, groups, rows, cols = q.shape
    count = k.shape[1] // rows
    heads = groups * cols // HD
    whole = pl.BlockSpec((1, groups, rows, cols), lambda s, j, p: (s, 0, 0, 0))
    kv_spec = pl.BlockSpec((1, rows, cols), lambda s, j, p: (s, jnp.minimum(j, p[0]), 0))
    out_spec = pl.BlockSpec((1, rows, cols), lambda s, j, p: (s, j, 0))
    return pl.pallas_call(
        functools.partial(attn_bwd_kernel, scale),
        grid_spec=pltpu.PrefetchScalarGridSpec(
            num_scalar_prefetch=1,
            grid=(seqs, count),
            in_specs=[
                whole,
                whole,
                whole,
                pl.BlockSpec((1, 8, heads * rows), lambda s, j, p: (s, 0, 0)),
                kv_spec,
                kv_spec,
            ],
            out_specs=[whole, out_spec, out_spec],
            scratch_shapes=[
                pltpu.VMEM((8, heads * rows), jnp.float32),
                pltpu.VMEM((groups, rows, cols), jnp.float32),
            ],
        ),
        out_shape=[
            jax.ShapeDtypeStruct(q.shape, jnp.float32),
            jax.ShapeDtypeStruct(k.shape, jnp.bfloat16),
            jax.ShapeDtypeStruct(k.shape, jnp.bfloat16),
        ],
        compiler_params=pltpu.CompilerParams(vmem_limit_bytes=VMEM_BYTES),
        name="attention_backward",
    )(place, q, g, o, logs, k, v)


def expert_kernel(x_ref, u_ref, share_ref, gate_ref, up_ref, down_ref, out_ref, copy_ref, pick_ref, hid_ref, sig_ref):
    x = x_ref[...]
    u = u_ref[...]
    experts, width = gate_ref.shape[0], gate_ref.shape[2]
    out = jnp.zeros(out_ref.shape, jnp.float32)
    copy = jnp.zeros(copy_ref.shape, jnp.float32)
    share_columns = jnp.transpose(share_ref[0])
    lane = lax.broadcasted_iota(jnp.int32, (x.shape[0], 128), 1)
    picks = jnp.zeros((x.shape[0], 128), jnp.float32)
    for e in range(experts):
        gate = dot_n(x, gate_ref[e])
        up = dot_n(x, up_ref[e])
        back = dot_t(u, down_ref[e])
        share = share_columns[:, e : e + 1]
        sig = 1.0 / (1.0 + jnp.exp(-gate))
        act = gate * sig
        hidden = act * up
        picks = jnp.where(lane == e, jnp.sum(hidden * back, axis=1, keepdims=True), picks)
        hidden_low = (hidden * share).astype(jnp.bfloat16)
        back = back * share
        gate_signal = (back * up * (sig * (1.0 + gate * (1.0 - sig)))).astype(jnp.bfloat16)
        up_signal = (back * act).astype(jnp.bfloat16)
        hid_ref[:, e * width : (e + 1) * width] = hidden_low
        sig_ref[:, (2 * e) * width : (2 * e + 1) * width] = gate_signal
        sig_ref[:, (2 * e + 1) * width : (2 * e + 2) * width] = up_signal
        out = out + dot_n(hidden_low, down_ref[e])
        copy = copy + dot_t(gate_signal, gate_ref[e]) + dot_t(up_signal, up_ref[e])
    out_ref[...] = out.astype(out_ref.dtype)
    copy_ref[...] = copy.astype(copy_ref.dtype)
    pick_ref[0] = jnp.transpose(picks)[: pick_ref.shape[1]]


def experts_both(x, u, shares, gate, up, down):
    tokens, model = x.shape
    tile = shares.shape[2]
    experts, _, width = gate.shape
    def rows(cols): return pl.BlockSpec((tile, cols), lambda t: (t, 0))
    def fixed(a): return pl.BlockSpec(a.shape, lambda t: (0,) * a.ndim, pipeline_mode=pl.Buffered(1))
    small = pl.BlockSpec((1,) + shares.shape[1:], lambda t: (t, 0, 0))
    return pl.pallas_call(
        expert_kernel,
        grid=(tokens // tile,),
        in_specs=[rows(model), rows(model), small, fixed(gate), fixed(up), fixed(down)],
        out_specs=[rows(model), rows(model), small, rows(experts * width), rows(2 * experts * width)],
        out_shape=[
            jax.ShapeDtypeStruct((tokens, model), jnp.bfloat16),
            jax.ShapeDtypeStruct((tokens, model), jnp.bfloat16),
            jax.ShapeDtypeStruct(shares.shape, jnp.float32),
            jax.ShapeDtypeStruct((tokens, experts * width), jnp.bfloat16),
            jax.ShapeDtypeStruct((tokens, 2 * experts * width), jnp.bfloat16),
        ],
        compiler_params=pltpu.CompilerParams(vmem_limit_bytes=VMEM_BYTES),
        name="experts_both",
    )(x, u, shares, gate, up, down)


def turned_kernel(left_ref, right_ref, out_ref):
    out_ref[...] = dot_c(left_ref[...], right_ref[...]).astype(out_ref.dtype)


def turned_product(left, right, rows):
    return pl.pallas_call(
        turned_kernel,
        grid=(left.shape[1] // rows,),
        in_specs=[
            pl.BlockSpec((left.shape[0], rows), lambda i: (0, i)),
            pl.BlockSpec(right.shape, lambda i: (0, 0), pipeline_mode=pl.Buffered(1)),
        ],
        out_specs=pl.BlockSpec((rows, right.shape[1]), lambda i: (i, 0)),
        out_shape=jax.ShapeDtypeStruct((left.shape[1], right.shape[1]), jnp.bfloat16),
        compiler_params=pltpu.CompilerParams(vmem_limit_bytes=VMEM_BYTES),
        name="turned_product",
    )(left, right)


MESH = pl.DeviceIdType.MESH


def greet(targets):
    barrier = pltpu.get_barrier_semaphore()
    awaited = 0
    for target, there in targets:
        if there is None:
            pl.semaphore_signal(barrier, inc=1, device_id=target, device_id_type=MESH)
            awaited = awaited + 1
        else:

            @pl.when(there)
            def _():
                pl.semaphore_signal(barrier, inc=1, device_id=target, device_id_type=MESH)

            awaited = awaited + jnp.where(there, 1, 0)
    pl.semaphore_wait(barrier, awaited)


def copier(source, target, sends, receives, number, device):
    return pltpu.make_async_remote_copy(
        src_ref=source,
        dst_ref=target,
        send_sem=sends.at[number],
        recv_sem=receives.at[number],
        device_id=device,
        device_id_type=MESH,
    )


def square_gather_kernel(x_ref, o_ref, local_sem, sends, receives):
    narrow, wide = lax.axis_index("narrow"), lax.axis_index("wide")
    rows = x_ref.shape[1]
    beside, across = jnp.bitwise_xor(narrow, 1), jnp.bitwise_xor(narrow, 2)
    corner = jnp.bitwise_xor(narrow, 3)
    to_beside, to_across = (beside, wide), (across, wide)
    greet([(to_beside, None), (to_across, None)])

    def place(half, owner):
        return o_ref.at[half, pl.ds(owner * rows, rows)]

    own = pltpu.make_async_copy(x_ref, o_ref.at[:, pl.ds(narrow * rows, rows)], local_sem)
    first = copier(x_ref.at[0], place(0, narrow), sends, receives, 0, to_beside)
    second = copier(x_ref.at[1], place(1, narrow), sends, receives, 1, to_across)
    third = copier(x_ref.at[1], place(1, narrow), sends, receives, 2, to_beside)
    fourth = copier(x_ref.at[0], place(0, narrow), sends, receives, 3, to_across)
    for copy in (first, second, third, fourth):
        copy.start()
    own.start()
    copier(x_ref.at[0], place(0, beside), sends, receives, 0, to_beside).wait_recv()
    fifth = copier(place(0, beside), place(0, beside), sends, receives, 4, to_across)
    fifth.start()
    copier(x_ref.at[1], place(1, across), sends, receives, 1, to_across).wait_recv()
    sixth = copier(place(1, across), place(1, across), sends, receives, 5, to_beside)
    sixth.start()
    copier(x_ref.at[1], place(1, beside), sends, receives, 2, to_beside).wait_recv()
    copier(x_ref.at[0], place(0, across), sends, receives, 3, to_across).wait_recv()
    copier(x_ref.at[0], place(0, corner), sends, receives, 4, to_across).wait_recv()
    copier(x_ref.at[1], place(1, corner), sends, receives, 5, to_beside).wait_recv()
    for copy in (first, second, third, fourth, fifth, sixth):
        copy.wait_send()
    own.wait()


def gather_narrow(block, number):
    count = lax.axis_size("narrow")
    if count != 4 or block.shape[0] != 2:
        return lax.all_gather(block, "narrow", axis=1, tiled=True)
    return pl.pallas_call(
        square_gather_kernel,
        out_shape=jax.ShapeDtypeStruct(
            (block.shape[0], count * block.shape[1], block.shape[2]), block.dtype
        ),
        in_specs=[pl.BlockSpec(memory_space=pl.ANY)],
        out_specs=pl.BlockSpec(memory_space=pl.ANY),
        scratch_shapes=[
            pltpu.SemaphoreType.DMA,
            pltpu.SemaphoreType.DMA((6,)),
            pltpu.SemaphoreType.DMA((6,)),
        ],
        compiler_params=pltpu.CompilerParams(collective_id=number, has_side_effects=True),
        name="square_gather",
    )(block)


def square_scatter_kernel(p_ref, o_ref, part_ref, sum_ref, in_ref, sends, receives):
    narrow, wide = lax.axis_index("narrow"), lax.axis_index("wide")
    rows = o_ref.shape[1]
    beside, across = jnp.bitwise_xor(narrow, 1), jnp.bitwise_xor(narrow, 2)
    corner = jnp.bitwise_xor(narrow, 3)
    to_beside, to_across = (beside, wide), (across, wide)
    greet([(to_beside, None), (to_across, None)])

    def mine(half, owner):
        return p_ref.at[half, pl.ds(owner * rows, rows)]

    first = copier(mine(0, corner), part_ref.at[0], sends, receives, 0, to_beside)
    second = copier(mine(1, corner), part_ref.at[1], sends, receives, 1, to_across)
    third = copier(mine(0, beside), in_ref.at[0, 0], sends, receives, 2, to_beside)
    fourth = copier(mine(1, across), in_ref.at[1, 1], sends, receives, 3, to_across)
    for copy in (first, second, third, fourth):
        copy.start()
    first.wait_recv()
    sum_ref[0] = (
        part_ref[0].astype(jnp.float32) + mine(0, across)[...].astype(jnp.float32)
    ).astype(sum_ref.dtype)
    fifth = copier(sum_ref.at[0], in_ref.at[1, 0], sends, receives, 4, to_across)
    fifth.start()
    second.wait_recv()
    sum_ref[1] = (
        part_ref[1].astype(jnp.float32) + mine(1, beside)[...].astype(jnp.float32)
    ).astype(sum_ref.dtype)
    sixth = copier(sum_ref.at[1], in_ref.at[0, 1], sends, receives, 5, to_beside)
    sixth.start()
    third.wait_recv()
    fifth.wait_recv()
    o_ref[0] = (
        mine(0, narrow)[...].astype(jnp.float32)
        + in_ref[0, 0].astype(jnp.float32)
        + in_ref[1, 0].astype(jnp.float32)
    )
    fourth.wait_recv()
    sixth.wait_recv()
    o_ref[1] = (
        mine(1, narrow)[...].astype(jnp.float32)
        + in_ref[0, 1].astype(jnp.float32)
        + in_ref[1, 1].astype(jnp.float32)
    )
    for copy in (first, second, third, fourth, fifth, sixth):
        copy.wait_send()


def scatter_narrow(partial, number):
    count = lax.axis_size("narrow")
    seqs, rows, cols = partial.shape
    if count != 4 or seqs != 2:
        return lax.psum_scatter(partial, "narrow", scatter_dimension=1, tiled=True).astype(
            jnp.float32
        )
    return pl.pallas_call(
        square_scatter_kernel,
        out_shape=jax.ShapeDtypeStruct((seqs, rows // count, cols), jnp.float32),
        in_specs=[pl.BlockSpec(memory_space=pltpu.VMEM)],
        out_specs=pl.BlockSpec(memory_space=pltpu.VMEM),
        scratch_shapes=[
            pltpu.VMEM((2, rows // count, cols), partial.dtype),
            pltpu.VMEM((2, rows // count, cols), partial.dtype),
            pltpu.VMEM((2, 2, rows // count, cols), partial.dtype),
            pltpu.SemaphoreType.DMA((6,)),
            pltpu.SemaphoreType.DMA((6,)),
        ],
        compiler_params=pltpu.CompilerParams(
            collective_id=number, has_side_effects=True, vmem_limit_bytes=VMEM_BYTES
        ),
        name="square_scatter",
    )(partial)


def line_places():
    narrow, wide = lax.axis_index("narrow"), lax.axis_index("wide")
    chips = lax.axis_size("wide") // 2
    chip, core = wide // 2, lax.rem(wide, 2)
    sibling = (narrow, wide + 1 - 2 * core)
    above = (narrow, jnp.minimum(wide + 2, 2 * chips - 2 + core))
    below = (narrow, jnp.maximum(wide - 2, core))
    return chips, chip, core, sibling, above, below


def line_gather_kernel(axes, falling, *refs):
    count = len(axes)
    x_refs, o_refs = refs[:count], refs[count : 2 * count]
    local_sem, core_s, core_r, up_s, up_r, down_s, down_r = refs[2 * count :]
    chips, chip, core, sibling, above, below = line_places()
    has_above, has_below = chip < chips - 1, chip > 0
    greet([(sibling, None), (above, has_above), (below, has_below)])

    def place(item, owner_chip, owner_core):
        axis = axes[item]
        size = x_refs[item].shape[axis]
        at = (owner_chip * 2 + owner_core) * size
        return o_refs[item].at[(slice(None),) * axis + (pl.ds(at, size),)]

    def send(item, source, owner_chip, sems, number, device):
        return copier(source, place(item, owner_chip, core), sems[0].at[item], sems[1].at[item], number, device)

    def arrival(item, owner_chip, owner_core, sems, number):
        spot = place(item, owner_chip, owner_core)
        return copier(spot, spot, sems[0].at[item], sems[1].at[item], number, sibling)

    ups, downs, cores = (up_s, up_r), (down_s, down_r), (core_s, core_r)
    for item in range(count):
        x_ref = x_refs[item]

        @pl.when(has_above)
        def _():
            send(item, x_ref, chip, ups, 1, above).start()

        if falling:

            @pl.when(has_below)
            def _():
                send(item, x_ref, chip, downs, 1, below).start()

        send(item, x_ref, chip, cores, 0, sibling).start()
        pltpu.make_async_copy(x_ref, place(item, chip, core), local_sem.at[item]).start()
    for step in range(1, chips):
        for item in range(count):

            @pl.when(chip >= step)
            def _():
                came = chip - step
                arrival(item, came, core, ups, step).wait_recv()
                spot = place(item, came, core)

                @pl.when(has_above)
                def _():
                    send(item, spot, came, ups, step + 1, above).start()

                send(item, spot, came, cores, step, sibling).start()

            if falling:

                @pl.when(chip + step < chips)
                def _():
                    came = chip + step
                    arrival(item, came, core, downs, step).wait_recv()
                    spot = place(item, came, core)

                    @pl.when(has_below)
                    def _():
                        send(item, spot, came, downs, step + 1, below).start()

                    send(item, spot, came, cores, chips - 1 + step, sibling).start()

    for item in range(count):
        for step in range(chips):

            @pl.when(chip >= step)
            def _():
                came = chip - step
                arrival(item, came, 1 - core, cores, step).wait_recv()
                arrival(item, came, core, cores, step).wait_send()

                @pl.when(has_above)
                def _():
                    arrival(item, came, core, ups, step + 1).wait_send()

            if falling:

                @pl.when(chip + step < chips)
                def _():
                    came = chip + step
                    if step:
                        arrival(item, came, 1 - core, cores, chips - 1 + step).wait_recv()
                        arrival(item, came, core, cores, chips - 1 + step).wait_send()

                    @pl.when(has_below)
                    def _():
                        arrival(item, came, core, downs, step + 1).wait_send()

        pltpu.make_async_copy(x_refs[item], place(item, chip, core), local_sem.at[item]).wait()


def gather_wide(blocks, axes, falling, number):
    wide_count = lax.axis_size("wide")
    chips = wide_count // 2
    count = len(blocks)

    def grown(block, axis):
        shape = list(block.shape)
        shape[axis] *= wide_count
        return jax.ShapeDtypeStruct(tuple(shape), block.dtype)

    sems = [pltpu.SemaphoreType.DMA((count, 2 * chips))] * 2
    sems += [pltpu.SemaphoreType.DMA((count, chips + 1))] * 4
    return pl.pallas_call(
        functools.partial(line_gather_kernel, axes, falling),
        out_shape=[grown(block, axis) for block, axis in zip(blocks, axes)],
        in_specs=[pl.BlockSpec(memory_space=pl.ANY)] * count,
        out_specs=[pl.BlockSpec(memory_space=pl.ANY)] * count,
        scratch_shapes=[pltpu.SemaphoreType.DMA((count,))] + sems,
        compiler_params=pltpu.CompilerParams(collective_id=number, has_side_effects=True),
        name="line_gather",
    )(*blocks)


def line_scatter_kernel(rising, count, *refs):
    p_refs, o_refs = refs[:count], refs[count : 2 * count]
    core_in = refs[2 * count : 3 * count]
    up_in, down_in = refs[3 * count : 4 * count], refs[4 * count : 5 * count]
    up_out, down_out = refs[5 * count : 6 * count], refs[6 * count : 7 * count]
    core_s, core_r, up_s, up_r, down_s, down_r = refs[7 * count :]
    chips, chip, core, sibling, above, below = line_places()
    has_above, has_below = chip < chips - 1, chip > 0
    greet([(sibling, None), (above, has_above), (below, has_below)])
    order = [step for step in range(chips - 1, -1, -1)]

    def core_copy(item, distance, target):
        return copier(
            p_refs[item].at[target * 2 + 1 - core],
            core_in[item].at[chips - 1 + distance],
            core_s.at[item],
            core_r.at[item],
            chips - 1 + distance,
            sibling,
        )

    def both_ways(action):
        for step in order:

            @pl.when(chip >= step)
            def _():
                action(-step, chip - step)

            if rising and step:

                @pl.when(chip + step < chips)
                def _():
                    action(step, chip + step)

    def start_core(distance, target):
        for item in range(count):
            core_copy(item, distance, target).start()

    both_ways(start_core)

    def own_sum(item, distance, target):
        core_copy(item, distance, target).wait_recv()
        return p_refs[item][target * 2 + core].astype(jnp.float32) + core_in[item][
            chips - 1 + distance
        ].astype(jnp.float32)

    def up_copy(item, distance):
        return copier(
            up_out[item].at[distance],
            up_in[item].at[distance - 1],
            up_s.at[item],
            up_r.at[item],
            distance - 1,
            above,
        )

    def down_copy(item, distance):
        return copier(
            down_out[item].at[distance],
            down_in[item].at[distance - 1],
            down_s.at[item],
            down_r.at[item],
            distance - 1,
            below,
        )

    def pass_on(distance, target):
        for item in range(count):
            total = own_sum(item, distance, target)
            if distance > 0:
                out, copy_of, arrived, more = up_out[item], up_copy, up_in[item], has_below
            else:
                out, copy_of, arrived, more = down_out[item], down_copy, down_in[item], has_above
            size = abs(distance)
            if size + 1 < chips:

                @pl.when(more)
                def _():
                    copy_of(item, size + 1).wait_recv()
                    out[size] = (total + arrived[size].astype(jnp.float32)).astype(out.dtype)

                @pl.when(jnp.logical_not(more))
                def _():
                    out[size] = total.astype(out.dtype)

            else:
                out[size] = total.astype(out.dtype)
            copy_of(item, size).start()

    for step in order[:-1]:

        @pl.when(chip >= step)
        def _():
            pass_on(-step, chip - step)

        if rising:

            @pl.when(chip + step < chips)
            def _():
                pass_on(step, chip + step)

    for item in range(count):
        o_refs[item][...] = own_sum(item, 0, chip)

        @pl.when(has_above)
        def _():
            down_copy(item, 1).wait_recv()
            o_refs[item][...] += down_in[item][0].astype(jnp.float32)

        if rising:

            @pl.when(has_below)
            def _():
                up_copy(item, 1).wait_recv()
                o_refs[item][...] += up_in[item][0].astype(jnp.float32)

    def finish(distance, target):
        for item in range(count):
            core_copy(item, distance, target).wait_send()
            if distance > 0:
                up_copy(item, distance).wait_send()
            if distance < 0:
                down_copy(item, -distance).wait_send()

    both_ways(finish)


def scatter_wide(partials, rising, number):
    chips = lax.axis_size("wide") // 2
    count = len(partials)

    def several(size):
        return [pltpu.VMEM((size,) + partial.shape[1:], partial.dtype) for partial in partials]

    sems = [pltpu.SemaphoreType.DMA((count, 2 * chips))] * 2
    sems += [pltpu.SemaphoreType.DMA((count, chips + 1))] * 4
    buffers = several(2 * chips - 1) + several(chips) * 2 + several(chips) * 2
    return pl.pallas_call(
        functools.partial(line_scatter_kernel, rising, count),
        out_shape=[jax.ShapeDtypeStruct(partial.shape[1:], jnp.float32) for partial in partials],
        in_specs=[pl.BlockSpec(memory_space=pltpu.VMEM)] * count,
        out_specs=[pl.BlockSpec(memory_space=pltpu.VMEM)] * count,
        scratch_shapes=buffers + sems,
        compiler_params=pltpu.CompilerParams(
            collective_id=number, has_side_effects=True, vmem_limit_bytes=VMEM_BYTES
        ),
        name="line_scatter",
    )(*partials)


def small_sum_kernel(steps, x_ref, o_ref, in_ref, out_ref, sends, receives):
    narrow, wide = lax.axis_index("narrow"), lax.axis_index("wide")
    partners = [
        (jnp.bitwise_xor(narrow, bit), wide) if axis else (narrow, jnp.bitwise_xor(wide, bit))
        for axis, bit in steps
    ]
    greet([(partner, None) for partner in partners])
    o_ref[...] = x_ref[...]
    for step, partner in enumerate(partners):
        out_ref[step] = o_ref[...]
        copy = copier(out_ref.at[step], in_ref.at[step], sends, receives, step, partner)
        copy.start()
        copy.wait_recv()
        o_ref[...] += in_ref[step]
    for step, partner in enumerate(partners):
        copier(out_ref.at[step], in_ref.at[step], sends, receives, step, partner).wait_send()


def small_sum(values, number):
    counts = (lax.axis_size("wide"), lax.axis_size("narrow"))
    steps = [
        (axis, 1 << bit) for axis in (1, 0) for bit in range(counts[axis].bit_length() - 1)
    ]
    return pl.pallas_call(
        functools.partial(small_sum_kernel, steps),
        out_shape=jax.ShapeDtypeStruct(values.shape, values.dtype),
        in_specs=[pl.BlockSpec(memory_space=pltpu.VMEM)],
        out_specs=pl.BlockSpec(memory_space=pltpu.VMEM),
        scratch_shapes=[
            pltpu.VMEM((len(steps),) + values.shape, values.dtype),
            pltpu.VMEM((len(steps),) + values.shape, values.dtype),
            pltpu.SemaphoreType.DMA((len(steps),)),
            pltpu.SemaphoreType.DMA((len(steps),)),
        ],
        compiler_params=pltpu.CompilerParams(
            collective_id=number, has_side_effects=True, vmem_limit_bytes=VMEM_BYTES
        ),
        name="small_sum",
    )(values)


def angles_of(positions, factor):
    half_size = HD // 2
    frequency = ROPE_BASE ** (-jnp.arange(half_size, dtype=jnp.float32) * 2.0 / HD)
    angles = (positions.astype(jnp.float32) / factor)[:, None] * frequency[None, :]
    return jnp.cos(angles), jnp.sin(angles)


def rotate(tensor, cosine, sine):
    half_size = tensor.shape[-1] // 2
    leading = tensor[..., :half_size]
    trailing = tensor[..., half_size:]
    return jnp.concatenate(
        [leading * cosine - trailing * sine, trailing * cosine + leading * sine], axis=-1
    )


def inverse_of(inputs):
    return lax.rsqrt(jnp.mean(inputs * inputs, axis=-1, keepdims=True) + EPSILON)


def normalize_back(inputs, inverse, gain_vector, upstream):
    scaled = inputs * inverse
    through = upstream * gain_vector
    input_grad = inverse * (through - scaled * jnp.mean(through * scaled, axis=-1, keepdims=True))
    gain_grad = jnp.sum(upstream * scaled, axis=(0, 1))
    return (input_grad, gain_grad)


def on_device(
    tokens,
    gain_attn,
    w_query,
    w_key,
    w_value,
    w_out,
    gain_moe,
    w_router,
    w_gate,
    w_up,
    w_down,
    routes,
    rope_scale,
    cotangent,
):
    narrow_count = lax.axis_size("narrow")
    wide_count = lax.axis_size("wide")
    wide_place = lax.axis_index("wide")
    local_rows, sequences, model_width = tokens.shape
    block_rows = local_rows * narrow_count
    query_cols = w_query.shape[1]
    kv_cols = w_key.shape[1]
    kv_heads = kv_cols // HD
    heads = query_cols // HD
    group_size = heads // kv_heads
    score_scale = HD ** (-0.5)
    factor = rope_scale[0]
    place = wide_place.astype(jnp.int32).reshape(1)
    token_count = local_rows * sequences

    token_float = tokens.swapaxes(0, 1).astype(jnp.float32)
    upstream_low = cotangent.swapaxes(0, 1)
    upstream = upstream_low.astype(jnp.float32)
    upstream_all = lax.all_gather(
        upstream_low.reshape(token_count, model_width), "wide", axis=0, tiled=True
    )

    attn_inverse = inverse_of(token_float)
    attn_low = (token_float * attn_inverse * gain_attn).astype(jnp.bfloat16)
    attn_block = gather_narrow(attn_low, 0)
    query_weight = w_query.reshape(model_width, kv_heads, group_size, HD).swapaxes(1, 2)
    joint_weight = jnp.concatenate(
        [query_weight.reshape(model_width, query_cols), w_key, w_value], axis=1
    )
    out_weight = w_out.reshape(kv_heads, group_size, HD, model_width).swapaxes(0, 1)
    out_weight = out_weight.reshape(query_cols, model_width)
    joint_proj = jnp.einsum(
        "std,dc->stc", attn_block, joint_weight, preferred_element_type=jnp.float32
    )
    cosine, sine = angles_of(wide_place * block_rows + lax.iota(jnp.int32, block_rows), factor)
    head_cosine, head_sine = cosine[None, :, None, :], sine[None, :, None, :]

    def by_group(flat):
        return flat.reshape(sequences, block_rows, group_size, kv_cols).swapaxes(1, 2)

    def flat_of(groups):
        return groups.swapaxes(1, 2).reshape(sequences, block_rows, query_cols)

    query_rot = rotate(
        joint_proj[..., :query_cols].reshape(sequences, block_rows, heads, HD),
        head_cosine,
        head_sine,
    ).astype(jnp.bfloat16)
    query_group = by_group(
        (query_rot * jnp.bfloat16(score_scale)).reshape(sequences, block_rows, query_cols)
    )
    key_rot = rotate(
        joint_proj[..., query_cols : query_cols + kv_cols].reshape(
            sequences, block_rows, kv_heads, HD
        ),
        head_cosine,
        head_sine,
    )
    key_local = key_rot.astype(jnp.bfloat16).reshape(sequences, block_rows, kv_cols)
    value_local = joint_proj[..., query_cols + kv_cols :].astype(jnp.bfloat16)
    (pair_all,) = gather_wide([jnp.stack([key_local, value_local])], (2,), False, 1)
    key_all, value_all = pair_all[0], pair_all[1]

    attn_result, attended, log_total = attn_fwd(
        place, query_group, key_all, value_all.swapaxes(1, 2)
    )
    out_low = flat_of(attended)
    attn_branch = scatter_narrow(
        jnp.einsum("stc,cd->std", out_low, out_weight, preferred_element_type=jnp.float32).astype(
            jnp.bfloat16
        ),
        2,
    )
    residual = token_float + attn_branch
    moe_inverse = inverse_of(residual)
    moe_low = (residual * moe_inverse * gain_moe).astype(jnp.bfloat16)
    moe_flat = moe_low.reshape(token_count, model_width)

    expert_count = w_router.shape[1]
    local_experts = w_gate.shape[0]
    first_expert = wide_place * local_experts
    expert_ids = routes.swapaxes(0, 1).reshape(token_count, -1)
    onehot = expert_ids[:, :, None] == lax.iota(jnp.int32, expert_count)[None, None, :]
    named = jnp.sum(onehot.astype(jnp.float32), axis=1)
    logits = jnp.dot(moe_flat, w_router, preferred_element_type=jnp.float32)
    masked = jnp.where(named > 0, logits, MASKED)
    powers = jnp.exp(masked - jnp.max(masked, axis=-1, keepdims=True)) * named
    shares = powers / jnp.sum(powers, axis=-1, keepdims=True)

    moe_all, shares_all = gather_wide([moe_flat, shares.T[None]], (0, 0), True, 3)
    own_shares = lax.dynamic_slice_in_dim(shares_all, first_expert, local_experts, 1)
    own_shares = jnp.pad(own_shares, ((0, 0), (0, 8 - local_experts), (0, 0)))
    part_out, part_copy, own_picks, hidden_shared, signals = experts_both(
        moe_all, upstream_all, own_shares, w_gate, w_up, w_down
    )
    part_picks = lax.dynamic_update_slice_in_dim(
        jnp.zeros_like(shares_all), own_picks[:, :local_experts], first_expert, 1
    )

    def by_block(rows):
        return rows.reshape((wide_count, rows.shape[0] // wide_count) + rows.shape[1:])

    copy_sum, picks = scatter_wide([by_block(part_copy), part_picks], True, 4)
    (moe_part,) = scatter_wide([by_block(part_out)], True, 5)
    layer_out = (residual + moe_part.reshape(residual.shape)).astype(jnp.bfloat16)

    joint_signal = turned_product(moe_all, signals, block_rows // 2)
    down_update = turned_product(hidden_shared, upstream_all, block_rows // 2)
    width = w_gate.shape[2]
    split = joint_signal.reshape(model_width, local_experts, 2, width)
    expert_grads = tuple(
        lax.psum_scatter(update, "narrow", scatter_dimension=1, tiled=True).astype(jnp.float32)
        for update in (
            split[:, :, 0].swapaxes(0, 1),
            split[:, :, 1].swapaxes(0, 1),
            down_update.reshape(local_experts, width, model_width),
        )
    )

    picks = picks.T
    logit_grads = shares * (picks - jnp.sum(shares * picks, axis=-1, keepdims=True))
    router_grads = jnp.dot(logit_grads.T, moe_flat.astype(jnp.float32), precision=PRECISE)
    moe_grads = jnp.dot(logit_grads, w_router.astype(jnp.float32).T, precision=PRECISE)
    moe_grads = moe_grads + copy_sum
    norm_grads, moe_gain = normalize_back(
        residual, moe_inverse, gain_moe, moe_grads.reshape(residual.shape)
    )
    residual_grads = upstream + norm_grads
    branch_all = gather_narrow(residual_grads.astype(jnp.bfloat16), 6)
    attended_grads = jnp.einsum(
        "std,cd->stc", branch_all, out_weight, preferred_element_type=jnp.float32
    ).astype(jnp.bfloat16)
    query_grads, key_part, value_part = attn_bwd(
        score_scale,
        place,
        query_group,
        by_group(attended_grads),
        attn_result,
        log_total,
        key_all,
        value_all,
    )
    out_update = jnp.einsum("stc,std->cd", out_low, branch_all, preferred_element_type=jnp.float32)
    pair_parts = jnp.stack([key_part, value_part]).reshape(
        2, sequences, wide_count, block_rows, kv_cols
    )
    (pair_own,) = scatter_wide([pair_parts.transpose(2, 0, 1, 3, 4)], False, 7)
    query_low = rotate(
        flat_of(query_grads).reshape(sequences, block_rows, heads, HD), head_cosine, -head_sine
    ).astype(jnp.bfloat16)
    key_low = rotate(
        pair_own[0].reshape(sequences, block_rows, kv_heads, HD),
        head_cosine,
        -head_sine,
    ).astype(jnp.bfloat16)
    joint_grads = jnp.concatenate(
        [
            query_low.reshape(sequences, block_rows, query_cols),
            key_low.reshape(sequences, block_rows, kv_cols),
            pair_own[1].astype(jnp.bfloat16),
        ],
        axis=-1,
    )
    joint_update = jnp.einsum(
        "std,stc->dc", attn_block, joint_grads, preferred_element_type=jnp.float32
    )
    attn_grads = scatter_narrow(
        jnp.einsum(
            "stc,dc->std", joint_grads, joint_weight, preferred_element_type=jnp.float32
        ).astype(jnp.bfloat16),
        8,
    )
    token_grads, attn_gain = normalize_back(token_float, attn_inverse, gain_attn, attn_grads)
    token_grads = residual_grads + token_grads
    weight_updates = jnp.concatenate([joint_update, out_update.T], axis=1).astype(jnp.bfloat16)
    (joint_summed,) = scatter_wide([by_block(weight_updates)], True, 9)
    out_summed = joint_summed[:, query_cols + 2 * kv_cols :]
    small_parts = jnp.concatenate([router_grads, moe_gain[None, :], attn_gain[None, :]], axis=0)
    small_parts = jnp.pad(small_parts, ((0, -small_parts.shape[0] % 8), (0, 0)))
    small_summed = small_sum(small_parts, 10)
    return (
        layer_out.swapaxes(0, 1),
        token_grads.swapaxes(0, 1),
        small_summed[expert_count + 1],
        joint_summed[:, :query_cols]
        .reshape(-1, group_size, kv_heads, HD)
        .swapaxes(1, 2)
        .reshape(-1, query_cols),
        joint_summed[:, query_cols : query_cols + kv_cols],
        joint_summed[:, query_cols + kv_cols : query_cols + 2 * kv_cols],
        out_summed.T.reshape(group_size, kv_heads, HD, -1).swapaxes(0, 1).reshape(query_cols, -1),
        small_summed[expert_count],
        small_summed[:expert_count].T,
        expert_grads[0],
        expert_grads[1],
        expert_grads[2],
    )


def solution(mesh):
    return jax.shard_map(
        on_device,
        mesh=mesh,
        in_specs=(
            P(("wide", "narrow"), None, None),
            P(),
            P(None, "narrow"),
            P(None, "narrow"),
            P(None, "narrow"),
            P("narrow", None),
            P(),
            P(),
            P("wide", None, None),
            P("wide", None, None),
            P("wide", None, None),
            P(("wide", "narrow"), None, None),
            P(),
            P(("wide", "narrow"), None, None),
        ),
        out_specs=(
            P(("wide", "narrow"), None, None),
            P(("wide", "narrow"), None, None),
            P(),
            P("wide", "narrow"),
            P("wide", "narrow"),
            P("wide", "narrow"),
            P("narrow", "wide"),
            P(),
            P(),
            P("wide", "narrow", None),
            P("wide", "narrow", None),
            P("wide", "narrow", None),
        ),
        check_vma=False,
    )
```

```python
import functools

import jax
import jax.numpy as jnp
from jax import lax
from jax.experimental import pallas as pl
from jax.experimental.pallas import tpu as pltpu
from jax.sharding import PartitionSpec as P

HD = 64


EPSILON = 1e-06
ROPE_BASE = 10000.0
MASKED = -1e30
PRECISE = lax.Precision.HIGHEST
VMEM_BYTES = 56 << 20


MESH = pl.DeviceIdType.MESH


def greet(targets):
    barrier = pltpu.get_barrier_semaphore()
    awaited = 0
    for target, there in targets:
        if there is None:
            pl.semaphore_signal(barrier, inc=1, device_id=target, device_id_type=MESH)
            awaited = awaited + 1
        else:

            @pl.when(there)
            def _():
                pl.semaphore_signal(barrier, inc=1, device_id=target, device_id_type=MESH)

            awaited = awaited + jnp.where(there, 1, 0)
    pl.semaphore_wait(barrier, awaited)


def copier(source, target, sends, receives, number, device):
    return pltpu.make_async_remote_copy(
        src_ref=source,
        dst_ref=target,
        send_sem=sends.at[number],
        recv_sem=receives.at[number],
        device_id=device,
        device_id_type=MESH,
    )


def square_gather_kernel(x_ref, o_ref, local_sem, sends, receives):
    narrow, wide = lax.axis_index("narrow"), lax.axis_index("wide")
    rows = x_ref.shape[1]
    beside, across = jnp.bitwise_xor(narrow, 1), jnp.bitwise_xor(narrow, 2)
    corner = jnp.bitwise_xor(narrow, 3)
    to_beside, to_across = (beside, wide), (across, wide)
    greet([(to_beside, None), (to_across, None)])

    def place(half, owner):
        return o_ref.at[half, pl.ds(owner * rows, rows)]

    own = pltpu.make_async_copy(x_ref, o_ref.at[:, pl.ds(narrow * rows, rows)], local_sem)
    first = copier(x_ref.at[0], place(0, narrow), sends, receives, 0, to_beside)
    second = copier(x_ref.at[1], place(1, narrow), sends, receives, 1, to_across)
    third = copier(x_ref.at[1], place(1, narrow), sends, receives, 2, to_beside)
    fourth = copier(x_ref.at[0], place(0, narrow), sends, receives, 3, to_across)
    for copy in (first, second, third, fourth):
        copy.start()
    own.start()
    copier(x_ref.at[0], place(0, beside), sends, receives, 0, to_beside).wait_recv()
    fifth = copier(place(0, beside), place(0, beside), sends, receives, 4, to_across)
    fifth.start()
    copier(x_ref.at[1], place(1, across), sends, receives, 1, to_across).wait_recv()
    sixth = copier(place(1, across), place(1, across), sends, receives, 5, to_beside)
    sixth.start()
    copier(x_ref.at[1], place(1, beside), sends, receives, 2, to_beside).wait_recv()
    copier(x_ref.at[0], place(0, across), sends, receives, 3, to_across).wait_recv()
    copier(x_ref.at[0], place(0, corner), sends, receives, 4, to_across).wait_recv()
    copier(x_ref.at[1], place(1, corner), sends, receives, 5, to_beside).wait_recv()
    for copy in (first, second, third, fourth, fifth, sixth):
        copy.wait_send()
    own.wait()


def gather_narrow(block, number):
    count = lax.axis_size("narrow")
    if count != 4 or block.shape[0] != 2:
        return lax.all_gather(block, "narrow", axis=1, tiled=True)
    return pl.pallas_call(
        square_gather_kernel,
        out_shape=jax.ShapeDtypeStruct(
            (block.shape[0], count * block.shape[1], block.shape[2]), block.dtype
        ),
        in_specs=[pl.BlockSpec(memory_space=pl.ANY)],
        out_specs=pl.BlockSpec(memory_space=pl.ANY),
        scratch_shapes=[
            pltpu.SemaphoreType.DMA,
            pltpu.SemaphoreType.DMA((6,)),
            pltpu.SemaphoreType.DMA((6,)),
        ],
        compiler_params=pltpu.CompilerParams(collective_id=number, has_side_effects=True),
        name="square_gather",
    )(block)


def square_scatter_kernel(p_ref, o_ref, part_ref, sum_ref, in_ref, sends, receives):
    narrow, wide = lax.axis_index("narrow"), lax.axis_index("wide")
    rows = o_ref.shape[1]
    beside, across = jnp.bitwise_xor(narrow, 1), jnp.bitwise_xor(narrow, 2)
    corner = jnp.bitwise_xor(narrow, 3)
    to_beside, to_across = (beside, wide), (across, wide)
    greet([(to_beside, None), (to_across, None)])

    def mine(half, owner):
        return p_ref.at[half, pl.ds(owner * rows, rows)]

    first = copier(mine(0, corner), part_ref.at[0], sends, receives, 0, to_beside)
    second = copier(mine(1, corner), part_ref.at[1], sends, receives, 1, to_across)
    third = copier(mine(0, beside), in_ref.at[0, 0], sends, receives, 2, to_beside)
    fourth = copier(mine(1, across), in_ref.at[1, 1], sends, receives, 3, to_across)
    for copy in (first, second, third, fourth):
        copy.start()
    first.wait_recv()
    sum_ref[0] = (
        part_ref[0].astype(jnp.float32) + mine(0, across)[...].astype(jnp.float32)
    ).astype(sum_ref.dtype)
    fifth = copier(sum_ref.at[0], in_ref.at[1, 0], sends, receives, 4, to_across)
    fifth.start()
    second.wait_recv()
    sum_ref[1] = (
        part_ref[1].astype(jnp.float32) + mine(1, beside)[...].astype(jnp.float32)
    ).astype(sum_ref.dtype)
    sixth = copier(sum_ref.at[1], in_ref.at[0, 1], sends, receives, 5, to_beside)
    sixth.start()
    third.wait_recv()
    fifth.wait_recv()
    o_ref[0] = (
        mine(0, narrow)[...].astype(jnp.float32)
        + in_ref[0, 0].astype(jnp.float32)
        + in_ref[1, 0].astype(jnp.float32)
    )
    fourth.wait_recv()
    sixth.wait_recv()
    o_ref[1] = (
        mine(1, narrow)[...].astype(jnp.float32)
        + in_ref[0, 1].astype(jnp.float32)
        + in_ref[1, 1].astype(jnp.float32)
    )
    for copy in (first, second, third, fourth, fifth, sixth):
        copy.wait_send()


def scatter_narrow(partial, number):
    count = lax.axis_size("narrow")
    seqs, rows, cols = partial.shape
    if count != 4 or seqs != 2:
        return lax.psum_scatter(partial, "narrow", scatter_dimension=1, tiled=True).astype(
            jnp.float32
        )
    return pl.pallas_call(
        square_scatter_kernel,
        out_shape=jax.ShapeDtypeStruct((seqs, rows // count, cols), jnp.float32),
        in_specs=[pl.BlockSpec(memory_space=pltpu.VMEM)],
        out_specs=pl.BlockSpec(memory_space=pltpu.VMEM),
        scratch_shapes=[
            pltpu.VMEM((2, rows // count, cols), partial.dtype),
            pltpu.VMEM((2, rows // count, cols), partial.dtype),
            pltpu.VMEM((2, 2, rows // count, cols), partial.dtype),
            pltpu.SemaphoreType.DMA((6,)),
            pltpu.SemaphoreType.DMA((6,)),
        ],
        compiler_params=pltpu.CompilerParams(
            collective_id=number, has_side_effects=True, vmem_limit_bytes=VMEM_BYTES
        ),
        name="square_scatter",
    )(partial)


def line_places():
    narrow, wide = lax.axis_index("narrow"), lax.axis_index("wide")
    chips = lax.axis_size("wide") // 2
    chip, core = wide // 2, lax.rem(wide, 2)
    sibling = (narrow, wide + 1 - 2 * core)
    above = (narrow, jnp.minimum(wide + 2, 2 * chips - 2 + core))
    below = (narrow, jnp.maximum(wide - 2, core))
    return chips, chip, core, sibling, above, below


def line_gather_kernel(axes, falling, *refs):
    count = len(axes)
    x_refs, o_refs = refs[:count], refs[count : 2 * count]
    local_sem, core_s, core_r, up_s, up_r, down_s, down_r = refs[2 * count :]
    chips, chip, core, sibling, above, below = line_places()
    has_above, has_below = chip < chips - 1, chip > 0
    greet([(sibling, None), (above, has_above), (below, has_below)])

    def place(item, owner_chip, owner_core):
        axis = axes[item]
        size = x_refs[item].shape[axis]
        at = (owner_chip * 2 + owner_core) * size
        return o_refs[item].at[(slice(None),) * axis + (pl.ds(at, size),)]

    def send(item, source, owner_chip, sems, number, device):
        return copier(source, place(item, owner_chip, core), sems[0].at[item], sems[1].at[item], number, device)

    def arrival(item, owner_chip, owner_core, sems, number):
        spot = place(item, owner_chip, owner_core)
        return copier(spot, spot, sems[0].at[item], sems[1].at[item], number, sibling)

    ups, downs, cores = (up_s, up_r), (down_s, down_r), (core_s, core_r)
    for item in range(count):
        x_ref = x_refs[item]

        @pl.when(has_above)
        def _():
            send(item, x_ref, chip, ups, 1, above).start()

        if falling:

            @pl.when(has_below)
            def _():
                send(item, x_ref, chip, downs, 1, below).start()

        send(item, x_ref, chip, cores, 0, sibling).start()
        pltpu.make_async_copy(x_ref, place(item, chip, core), local_sem.at[item]).start()
    for step in range(1, chips):
        for item in range(count):

            @pl.when(chip >= step)
            def _():
                came = chip - step
                arrival(item, came, core, ups, step).wait_recv()
                spot = place(item, came, core)

                @pl.when(has_above)
                def _():
                    send(item, spot, came, ups, step + 1, above).start()

                send(item, spot, came, cores, step, sibling).start()

            if falling:

                @pl.when(chip + step < chips)
                def _():
                    came = chip + step
                    arrival(item, came, core, downs, step).wait_recv()
                    spot = place(item, came, core)

                    @pl.when(has_below)
                    def _():
                        send(item, spot, came, downs, step + 1, below).start()

                    send(item, spot, came, cores, chips - 1 + step, sibling).start()

    for item in range(count):
        for step in range(chips):

            @pl.when(chip >= step)
            def _():
                came = chip - step
                arrival(item, came, 1 - core, cores, step).wait_recv()
                arrival(item, came, core, cores, step).wait_send()

                @pl.when(has_above)
                def _():
                    arrival(item, came, core, ups, step + 1).wait_send()

            if falling:

                @pl.when(chip + step < chips)
                def _():
                    came = chip + step
                    if step:
                        arrival(item, came, 1 - core, cores, chips - 1 + step).wait_recv()
                        arrival(item, came, core, cores, chips - 1 + step).wait_send()

                    @pl.when(has_below)
                    def _():
                        arrival(item, came, core, downs, step + 1).wait_send()

        pltpu.make_async_copy(x_refs[item], place(item, chip, core), local_sem.at[item]).wait()


def gather_wide(blocks, axes, falling, number):
    wide_count = lax.axis_size("wide")
    chips = wide_count // 2
    count = len(blocks)

    def grown(block, axis):
        shape = list(block.shape)
        shape[axis] *= wide_count
        return jax.ShapeDtypeStruct(tuple(shape), block.dtype)

    sems = [pltpu.SemaphoreType.DMA((count, 2 * chips))] * 2
    sems += [pltpu.SemaphoreType.DMA((count, chips + 1))] * 4
    return pl.pallas_call(
        functools.partial(line_gather_kernel, axes, falling),
        out_shape=[grown(block, axis) for block, axis in zip(blocks, axes)],
        in_specs=[pl.BlockSpec(memory_space=pl.ANY)] * count,
        out_specs=[pl.BlockSpec(memory_space=pl.ANY)] * count,
        scratch_shapes=[pltpu.SemaphoreType.DMA((count,))] + sems,
        compiler_params=pltpu.CompilerParams(collective_id=number, has_side_effects=True),
        name="line_gather",
    )(*blocks)


def line_scatter_kernel(rising, count, *refs):
    p_refs, o_refs = refs[:count], refs[count : 2 * count]
    core_in = refs[2 * count : 3 * count]
    up_in, down_in = refs[3 * count : 4 * count], refs[4 * count : 5 * count]
    up_out, down_out = refs[5 * count : 6 * count], refs[6 * count : 7 * count]
    core_s, core_r, up_s, up_r, down_s, down_r = refs[7 * count :]
    chips, chip, core, sibling, above, below = line_places()
    has_above, has_below = chip < chips - 1, chip > 0
    greet([(sibling, None), (above, has_above), (below, has_below)])
    order = [step for step in range(chips - 1, -1, -1)]

    def core_copy(item, distance, target):
        return copier(
            p_refs[item].at[target * 2 + 1 - core],
            core_in[item].at[chips - 1 + distance],
            core_s.at[item],
            core_r.at[item],
            chips - 1 + distance,
            sibling,
        )

    def both_ways(action):
        for step in order:

            @pl.when(chip >= step)
            def _():
                action(-step, chip - step)

            if rising and step:

                @pl.when(chip + step < chips)
                def _():
                    action(step, chip + step)

    def start_core(distance, target):
        for item in range(count):
            core_copy(item, distance, target).start()

    both_ways(start_core)

    def own_sum(item, distance, target):
        core_copy(item, distance, target).wait_recv()
        return p_refs[item][target * 2 + core].astype(jnp.float32) + core_in[item][
            chips - 1 + distance
        ].astype(jnp.float32)

    def up_copy(item, distance):
        return copier(
            up_out[item].at[distance],
            up_in[item].at[distance - 1],
            up_s.at[item],
            up_r.at[item],
            distance - 1,
            above,
        )

    def down_copy(item, distance):
        return copier(
            down_out[item].at[distance],
            down_in[item].at[distance - 1],
            down_s.at[item],
            down_r.at[item],
            distance - 1,
            below,
        )

    def pass_on(distance, target):
        for item in range(count):
            total = own_sum(item, distance, target)
            if distance > 0:
                out, copy_of, arrived, more = up_out[item], up_copy, up_in[item], has_below
            else:
                out, copy_of, arrived, more = down_out[item], down_copy, down_in[item], has_above
            size = abs(distance)
            if size + 1 < chips:

                @pl.when(more)
                def _():
                    copy_of(item, size + 1).wait_recv()
                    out[size] = (total + arrived[size].astype(jnp.float32)).astype(out.dtype)

                @pl.when(jnp.logical_not(more))
                def _():
                    out[size] = total.astype(out.dtype)

            else:
                out[size] = total.astype(out.dtype)
            copy_of(item, size).start()

    for step in order[:-1]:

        @pl.when(chip >= step)
        def _():
            pass_on(-step, chip - step)

        if rising:

            @pl.when(chip + step < chips)
            def _():
                pass_on(step, chip + step)

    for item in range(count):
        o_refs[item][...] = own_sum(item, 0, chip)

        @pl.when(has_above)
        def _():
            down_copy(item, 1).wait_recv()
            o_refs[item][...] += down_in[item][0].astype(jnp.float32)

        if rising:

            @pl.when(has_below)
            def _():
                up_copy(item, 1).wait_recv()
                o_refs[item][...] += up_in[item][0].astype(jnp.float32)

    def finish(distance, target):
        for item in range(count):
            core_copy(item, distance, target).wait_send()
            if distance > 0:
                up_copy(item, distance).wait_send()
            if distance < 0:
                down_copy(item, -distance).wait_send()

    both_ways(finish)


def scatter_wide(partials, rising, number):
    chips = lax.axis_size("wide") // 2
    count = len(partials)

    def several(size):
        return [pltpu.VMEM((size,) + partial.shape[1:], partial.dtype) for partial in partials]

    sems = [pltpu.SemaphoreType.DMA((count, 2 * chips))] * 2
    sems += [pltpu.SemaphoreType.DMA((count, chips + 1))] * 4
    buffers = several(2 * chips - 1) + several(chips) * 2 + several(chips) * 2
    return pl.pallas_call(
        functools.partial(line_scatter_kernel, rising, count),
        out_shape=[jax.ShapeDtypeStruct(partial.shape[1:], jnp.float32) for partial in partials],
        in_specs=[pl.BlockSpec(memory_space=pltpu.VMEM)] * count,
        out_specs=[pl.BlockSpec(memory_space=pltpu.VMEM)] * count,
        scratch_shapes=buffers + sems,
        compiler_params=pltpu.CompilerParams(
            collective_id=number, has_side_effects=True, vmem_limit_bytes=VMEM_BYTES
        ),
        name="line_scatter",
    )(*partials)


def small_sum_kernel(steps, x_ref, o_ref, in_ref, out_ref, sends, receives):
    narrow, wide = lax.axis_index("narrow"), lax.axis_index("wide")
    partners = [
        (jnp.bitwise_xor(narrow, bit), wide) if axis else (narrow, jnp.bitwise_xor(wide, bit))
        for axis, bit in steps
    ]
    greet([(partner, None) for partner in partners])
    o_ref[...] = x_ref[...]
    for step, partner in enumerate(partners):
        out_ref[step] = o_ref[...]
        copy = copier(out_ref.at[step], in_ref.at[step], sends, receives, step, partner)
        copy.start()
        copy.wait_recv()
        o_ref[...] += in_ref[step]
    for step, partner in enumerate(partners):
        copier(out_ref.at[step], in_ref.at[step], sends, receives, step, partner).wait_send()


def small_sum(values, number):
    counts = (lax.axis_size("wide"), lax.axis_size("narrow"))
    steps = [
        (axis, 1 << bit) for axis in (1, 0) for bit in range(counts[axis].bit_length() - 1)
    ]
    return pl.pallas_call(
        functools.partial(small_sum_kernel, steps),
        out_shape=jax.ShapeDtypeStruct(values.shape, values.dtype),
        in_specs=[pl.BlockSpec(memory_space=pltpu.VMEM)],
        out_specs=pl.BlockSpec(memory_space=pltpu.VMEM),
        scratch_shapes=[
            pltpu.VMEM((len(steps),) + values.shape, values.dtype),
            pltpu.VMEM((len(steps),) + values.shape, values.dtype),
            pltpu.SemaphoreType.DMA((len(steps),)),
            pltpu.SemaphoreType.DMA((len(steps),)),
        ],
        compiler_params=pltpu.CompilerParams(
            collective_id=number, has_side_effects=True, vmem_limit_bytes=VMEM_BYTES
        ),
        name="small_sum",
    )(values)


def dot_t(left, right):
    return lax.dot_general(left, right, (((1,), (1,)), ((), ())), preferred_element_type=jnp.float32)


def dot_n(left, right):
    return lax.dot_general(left, right, (((1,), (0,)), ((), ())), preferred_element_type=jnp.float32)


def dot_c(left, right):
    return lax.dot_general(left, right, (((0,), (0,)), ((), ())), preferred_element_type=jnp.float32)


def head_mask(shape, head):
    lane = lax.broadcasted_iota(jnp.int32, shape, len(shape) - 1)
    return jnp.logical_and(lane >= head * HD, lane < (head + 1) * HD)


def only_head(block, head):
    if block.shape[-1] == HD:
        return block
    return jnp.where(head_mask(block.shape, head), block, jnp.zeros_like(block))


def pairs_of(q_ref, cols):
    return [
        (group, head) for group in range(q_ref.shape[2] // cols) for head in range(cols // HD)
    ]


def causal(shape):
    row = lax.broadcasted_iota(jnp.int32, shape, 0)
    col = lax.broadcasted_iota(jnp.int32, shape, 1)
    return row <= col


def attn_fwd_kernel(
    q_ref, pair_ref, held_ref, o_ref, low_ref, log_ref, top_ref, sum_ref, acc_ref, *sems
):
    local_sem, core_s, core_r, up_s, up_r = sems
    chips, chip, core, sibling, above, below = line_places()
    has_above, has_below = chip < chips - 1, chip > 0
    greet([(sibling, None), (above, has_above), (below, has_below)])
    seqs, rows, _ = q_ref.shape
    cols = pair_ref.shape[2] // 2
    pairs = pairs_of(q_ref, cols)
    own = chip * 2 + core

    def up_copy(source, block, number):
        return copier(source, held_ref.at[block], up_s, up_r, number, above)

    def core_copy(source, block, number):
        return copier(source, held_ref.at[block], core_s, core_r, number, sibling)

    @pl.when(has_above)
    def _():
        up_copy(pair_ref, own, 1).start()

    core_copy(pair_ref, own, 0).start()
    keep = pltpu.make_async_copy(pair_ref, held_ref.at[own], local_sem)
    keep.start()
    top_ref[...] = jnp.full(top_ref.shape, MASKED, jnp.float32)
    sum_ref[...] = jnp.zeros(sum_ref.shape, jnp.float32)
    acc_ref[...] = jnp.zeros(acc_ref.shape, jnp.float32)

    def one(pair_block, seq, masked):
        key_block = pair_block[:, :cols]
        value_turned = jnp.transpose(pair_block[:, cols:])

        def scores_of(number):
            group, head = pairs[number]
            return dot_t(key_block, only_head(q_ref[seq, :, pl.ds(group * cols, cols)], head))

        ahead = scores_of(0)
        for number, (group, head) in enumerate(pairs):
            part = pl.ds(number * rows, rows)
            lanes = pl.ds(head * HD, HD)
            scores = ahead
            if number + 1 < len(pairs):
                ahead = scores_of(number + 1)
            if masked:
                scores = jnp.where(causal(scores.shape), scores, MASKED)
            old = top_ref[seq, :1, part]
            new = jnp.maximum(old, jnp.max(scores, axis=0, keepdims=True))
            fade = jnp.exp(old - new)
            weights = jnp.exp(scores - new)
            sum_ref[seq, :1, part] = sum_ref[seq, :1, part] * fade + jnp.sum(
                weights, axis=0, keepdims=True
            )
            acc_ref[seq, group, lanes, :] = acc_ref[seq, group, lanes, :] * fade + dot_n(
                value_turned[head * HD : (head + 1) * HD, :], weights.astype(jnp.bfloat16)
            )
            top_ref[seq, :1, part] = new

    def block_of(block):
        def body(seq, carried):
            one(held_ref[block, seq], seq, False)
            return carried

        lax.fori_loop(0, seqs, body, 0)

    def own_body(seq, carried):
        one(pair_ref[seq], seq, True)
        return carried

    lax.fori_loop(0, seqs, own_body, 0)
    core_copy(pair_ref, chip * 2 + 1 - core, 0).wait_recv()

    @pl.when(core == 1)
    def _():
        block_of(own - 1)

    def step_body(step, carried):
        @pl.when(chip >= step)
        def _():
            came = (chip - step) * 2 + core
            other = (chip - step) * 2 + 1 - core
            up_copy(held_ref.at[came], came, step).wait_recv()

            @pl.when(has_above)
            def _():
                up_copy(held_ref.at[came], came, step + 1).start()

            core_copy(held_ref.at[came], came, step).start()
            block_of(came)
            core_copy(held_ref.at[other], other, step).wait_recv()
            block_of(other)

        return carried

    lax.fori_loop(1, chips, step_body, 0)

    def finish_body(seq, carried):
        for number, (group, head) in enumerate(pairs):
            part = pl.ds(number * rows, rows)
            lanes = pl.ds(head * HD, HD)
            total = sum_ref[seq, :1, part]
            acc_ref[seq, group, lanes, :] = acc_ref[seq, group, lanes, :] / total
            log_ref[seq, :, part] = jnp.broadcast_to(
                top_ref[seq, :1, part] + jnp.log(total), (8, rows)
            )
        for group in range(len(pairs) * HD // cols):
            result = jnp.transpose(acc_ref[seq, group])
            o_ref[seq, :, pl.ds(group * cols, cols)] = result
            low_ref[seq, :, pl.ds(group * cols, cols)] = result.astype(jnp.bfloat16)
        return carried

    lax.fori_loop(0, seqs, finish_body, 0)

    def sent_body(step, carried):
        @pl.when(chip >= step)
        def _():
            came = (chip - step) * 2 + core
            core_copy(held_ref.at[came], came, step).wait_send()

            @pl.when(has_above)
            def _():
                up_copy(held_ref.at[came], came, step + 1).wait_send()

        return carried

    lax.fori_loop(0, chips, sent_body, 0)
    keep.wait()


def attn_fwd(q, pair, number):
    seqs, rows, query_cols = q.shape
    cols = pair.shape[2] // 2
    wide_count = lax.axis_size("wide")
    chips = wide_count // 2
    heads = query_cols // HD
    whole = pl.BlockSpec(memory_space=pltpu.VMEM)
    return pl.pallas_call(
        attn_fwd_kernel,
        in_specs=[whole, whole],
        out_specs=[whole] * 4,
        out_shape=[
            jax.ShapeDtypeStruct((wide_count,) + pair.shape, pair.dtype),
            jax.ShapeDtypeStruct(q.shape, jnp.float32),
            jax.ShapeDtypeStruct(q.shape, jnp.bfloat16),
            jax.ShapeDtypeStruct((seqs, 8, heads * rows), jnp.float32),
        ],
        scratch_shapes=[
            pltpu.VMEM((seqs, 8, heads * rows), jnp.float32),
            pltpu.VMEM((seqs, 8, heads * rows), jnp.float32),
            pltpu.VMEM((seqs, query_cols // cols, cols, rows), jnp.float32),
            pltpu.SemaphoreType.DMA,
        ]
        + [pltpu.SemaphoreType.DMA((chips + 1,))] * 4,
        compiler_params=pltpu.CompilerParams(
            collective_id=number, has_side_effects=True, vmem_limit_bytes=VMEM_BYTES
        ),
        name="attention_forward",
    )(q, pair)


def attn_bwd_kernel(
    scale,
    q_ref,
    g_ref,
    o_ref,
    log_ref,
    held_ref,
    dq_ref,
    own_ref,
    inner_ref,
    mine_ref,
    core_out,
    core_in,
    down_out,
    down_in,
    core_s,
    core_r,
    down_s,
    down_r,
):
    chips, chip, core, sibling, above, below = line_places()
    has_above, has_below = chip < chips - 1, chip > 0
    greet([(sibling, None), (above, has_above), (below, has_below)])
    seqs, rows, _ = q_ref.shape
    cols = held_ref.shape[3] // 2
    pairs = pairs_of(q_ref, cols)

    def core_copy(step):
        return copier(core_out.at[step], core_in.at[step], core_s, core_r, step, sibling)

    def down_copy(step):
        return copier(down_out.at[step], down_in.at[step - 1], down_s, down_r, step - 1, below)

    def start_body(seq, carried):
        ones = jnp.ones((8, cols), jnp.float32)
        for number, (group, head) in enumerate(pairs):
            at = pl.ds(group * cols, cols)
            prod = only_head(g_ref[seq, :, at].astype(jnp.float32) * o_ref[seq, :, at], head)
            inner_ref[seq, :, pl.ds(number * rows, rows)] = lax.dot_general(
                ones,
                prod,
                (((1,), (1,)), ((), ())),
                precision=PRECISE,
                preferred_element_type=jnp.float32,
            )
        return carried

    lax.fori_loop(0, seqs, start_body, 0)
    dq_ref[...] = jnp.zeros(dq_ref.shape, jnp.float32)

    def one(block, seq, masked):
        key_block = held_ref[block, seq, :, :cols]
        value_block = held_ref[block, seq, :, cols:]
        dk = jnp.zeros(key_block.shape, jnp.float32)
        dv = jnp.zeros(key_block.shape, jnp.float32)

        def ahead_of(number):
            group, head = pairs[number]
            at = pl.ds(group * cols, cols)
            q = only_head(q_ref[seq, :, at], head)
            g = only_head(g_ref[seq, :, at], head)
            return q, g, dot_t(key_block, q), dot_t(value_block, g)

        ahead = ahead_of(0)
        for number, (group, head) in enumerate(pairs):
            part = pl.ds(number * rows, rows)
            at = pl.ds(group * cols, cols)
            q, g, scores, back = ahead
            if number + 1 < len(pairs):
                ahead = ahead_of(number + 1)
            probs = jnp.exp(scores - log_ref[seq, :1, part])
            if masked:
                probs = jnp.where(causal(scores.shape), probs, 0.0)
            grads = (probs * (back - inner_ref[seq, :1, part])).astype(jnp.bfloat16)
            dv = dv + dot_n(probs.astype(jnp.bfloat16), g)
            dk = dk + dot_n(grads, q)
            dq_ref[seq, :, at] = dq_ref[seq, :, at] + dot_c(grads, only_head(key_block, head))
        return dk, dv

    def block_into(block, out_ref, step, masked):
        def body(seq, carried):
            dk, dv = one(block, seq, masked)
            out_ref[step, seq] = jnp.concatenate([dk, dv], axis=1).astype(out_ref.dtype)
            return carried

        lax.fori_loop(0, seqs, body, 0)

    def pass_on(step):
        core_copy(step).wait_recv()
        mine_ref[step] = mine_ref[step] + core_in[step].astype(jnp.float32)

        @pl.when(has_above)
        def _():
            down_copy(step + 1).wait_recv()
            mine_ref[step] = mine_ref[step] + down_in[step].astype(jnp.float32)

        down_out[step] = mine_ref[step].astype(down_out.dtype)
        down_copy(step).start()

    def step_body(number, carried):
        step = chips - 1 - number

        @pl.when(chip >= step)
        def _():
            target = (chip - step) * 2
            block_into(target + 1 - core, core_out, step, False)
            core_copy(step).start()
            block_into(target + core, mine_ref, step, False)

        @pl.when(jnp.logical_and(has_above, chip >= step + 1))
        def _():
            pass_on(step + 1)

        @pl.when(jnp.logical_and(jnp.logical_not(has_above), chip >= step))
        def _():
            pass_on(step)

        return carried

    lax.fori_loop(0, chips - 1, step_body, 0)

    @pl.when(core == 1)
    def _():
        block_into(chip * 2, core_out, 0, False)
        core_copy(0).start()

    block_into(chip * 2 + core, mine_ref, 0, True)

    @pl.when(jnp.logical_and(has_above, chip >= 1))
    def _():
        pass_on(1)

    @pl.when(core == 0)
    def _():
        core_copy(0).wait_recv()
        mine_ref[0] = mine_ref[0] + core_in[0].astype(jnp.float32)

    @pl.when(has_above)
    def _():
        down_copy(1).wait_recv()
        mine_ref[0] = mine_ref[0] + down_in[0].astype(jnp.float32)

    own_ref[...] = mine_ref[0]
    dq_ref[...] = dq_ref[...] * scale

    @pl.when(core == 1)
    def _():
        core_copy(0).wait_send()

    def sent_body(step, carried):
        @pl.when(chip >= step)
        def _():
            core_copy(step).wait_send()
            down_copy(step).wait_send()

        return carried

    lax.fori_loop(1, chips, sent_body, 0)


def attn_bwd(scale, q, g, o, logs, held, number):
    seqs, rows, query_cols = q.shape
    chips = lax.axis_size("wide") // 2
    heads = query_cols // HD
    whole = pl.BlockSpec(memory_space=pltpu.VMEM)
    block = (chips,) + held.shape[1:]
    return pl.pallas_call(
        functools.partial(attn_bwd_kernel, scale),
        in_specs=[whole] * 5,
        out_specs=[whole] * 2,
        out_shape=[
            jax.ShapeDtypeStruct(q.shape, jnp.float32),
            jax.ShapeDtypeStruct(held.shape[1:], jnp.float32),
        ],
        scratch_shapes=[
            pltpu.VMEM((seqs, 8, heads * rows), jnp.float32),
            pltpu.VMEM(block, jnp.float32),
        ]
        + [pltpu.VMEM(block, jnp.bfloat16)] * 4
        + [pltpu.SemaphoreType.DMA((chips,))] * 4,
        compiler_params=pltpu.CompilerParams(
            collective_id=number, has_side_effects=True, vmem_limit_bytes=VMEM_BYTES
        ),
        name="attention_backward",
    )(q, g, o, logs, held)


def expert_kernel(x_ref, u_ref, share_ref, gate_ref, up_ref, down_ref, out_ref, copy_ref, pick_ref, hid_ref, sig_ref):
    x = x_ref[...]
    u = u_ref[...]
    experts, width = gate_ref.shape[0], gate_ref.shape[2]
    out = jnp.zeros(out_ref.shape, jnp.float32)
    copy = jnp.zeros(copy_ref.shape, jnp.float32)
    share_columns = jnp.transpose(share_ref[0])
    lane = lax.broadcasted_iota(jnp.int32, (x.shape[0], 128), 1)
    picks = jnp.zeros((x.shape[0], 128), jnp.float32)
    for e in range(experts):
        gate = dot_n(x, gate_ref[e])
        up = dot_n(x, up_ref[e])
        back = dot_t(u, down_ref[e])
        share = share_columns[:, e : e + 1]
        sig = 1.0 / (1.0 + jnp.exp(-gate))
        act = gate * sig
        hidden = act * up
        picks = jnp.where(lane == e, jnp.sum(hidden * back, axis=1, keepdims=True), picks)
        hidden_low = (hidden * share).astype(jnp.bfloat16)
        back = back * share
        gate_signal = (back * up * (sig * (1.0 + gate * (1.0 - sig)))).astype(jnp.bfloat16)
        up_signal = (back * act).astype(jnp.bfloat16)
        hid_ref[:, e * width : (e + 1) * width] = hidden_low
        sig_ref[:, e * width : (e + 1) * width] = gate_signal
        sig_ref[:, (experts + e) * width : (experts + e + 1) * width] = up_signal
        out = out + dot_n(hidden_low, down_ref[e])
        copy = copy + dot_t(gate_signal, gate_ref[e]) + dot_t(up_signal, up_ref[e])
    out_ref[...] = out.astype(out_ref.dtype)
    copy_ref[...] = copy.astype(copy_ref.dtype)
    pick_ref[0] = jnp.transpose(picks)[: pick_ref.shape[1]]


def experts_both(x, u, shares, gate, up, down):
    tokens, model = x.shape
    tile = shares.shape[2]
    experts, _, width = gate.shape
    def rows(cols): return pl.BlockSpec((tile, cols), lambda t: (t, 0))
    def fixed(a): return pl.BlockSpec(a.shape, lambda t: (0,) * a.ndim, pipeline_mode=pl.Buffered(1))
    small = pl.BlockSpec((1,) + shares.shape[1:], lambda t: (t, 0, 0))
    return pl.pallas_call(
        expert_kernel,
        grid=(tokens // tile,),
        in_specs=[rows(model), rows(model), small, fixed(gate), fixed(up), fixed(down)],
        out_specs=[rows(model), rows(model), small, rows(experts * width), rows(2 * experts * width)],
        out_shape=[
            jax.ShapeDtypeStruct((tokens, model), jnp.bfloat16),
            jax.ShapeDtypeStruct((tokens, model), jnp.bfloat16),
            jax.ShapeDtypeStruct(shares.shape, jnp.float32),
            jax.ShapeDtypeStruct((tokens, experts * width), jnp.bfloat16),
            jax.ShapeDtypeStruct((tokens, 2 * experts * width), jnp.bfloat16),
        ],
        compiler_params=pltpu.CompilerParams(vmem_limit_bytes=VMEM_BYTES),
        name="experts_both",
    )(x, u, shares, gate, up, down)


def turned_kernel(left_ref, right_ref, *out_refs):
    product = dot_c(left_ref[...], right_ref[...])
    at = 0
    for out_ref in out_refs:
        for part in range(out_ref.shape[0]):
            out_ref[part] = product[:, at : at + out_ref.shape[2]].astype(out_ref.dtype)
            at += out_ref.shape[2]


def turned_product(left, right, rows, kinds, parts):
    cols = right.shape[1] // (kinds * parts)
    return pl.pallas_call(
        turned_kernel,
        grid=(left.shape[1] // rows,),
        in_specs=[
            pl.BlockSpec((left.shape[0], rows), lambda i: (0, i)),
            pl.BlockSpec(right.shape, lambda i: (0, 0), pipeline_mode=pl.Buffered(1)),
        ],
        out_specs=[pl.BlockSpec((parts, rows, cols), lambda i: (0, i, 0))] * kinds,
        out_shape=[jax.ShapeDtypeStruct((parts, left.shape[1], cols), jnp.bfloat16)] * kinds,
        compiler_params=pltpu.CompilerParams(vmem_limit_bytes=VMEM_BYTES),
        name="turned_product",
    )(left, right)


def angles_of(positions, factor):
    half_size = HD // 2
    frequency = ROPE_BASE ** (-jnp.arange(half_size, dtype=jnp.float32) * 2.0 / HD)
    angles = (positions.astype(jnp.float32) / factor)[:, None] * frequency[None, :]
    return jnp.cos(angles), jnp.sin(angles)


def rotate(tensor, cosine, sine):
    half_size = tensor.shape[-1] // 2
    leading = tensor[..., :half_size]
    trailing = tensor[..., half_size:]
    return jnp.concatenate(
        [leading * cosine - trailing * sine, trailing * cosine + leading * sine], axis=-1
    )


def inverse_of(inputs):
    return lax.rsqrt(jnp.mean(inputs * inputs, axis=-1, keepdims=True) + EPSILON)


def normalize_back(inputs, inverse, gain_vector, upstream):
    scaled = inputs * inverse
    through = upstream * gain_vector
    input_grad = inverse * (through - scaled * jnp.mean(through * scaled, axis=-1, keepdims=True))
    gain_grad = jnp.sum(upstream * scaled, axis=(0, 1))
    return (input_grad, gain_grad)


def on_device(
    tokens,
    gain_attn,
    w_query,
    w_key,
    w_value,
    w_out,
    gain_moe,
    w_router,
    w_gate,
    w_up,
    w_down,
    routes,
    rope_scale,
    cotangent,
):
    narrow_count = lax.axis_size("narrow")
    wide_count = lax.axis_size("wide")
    wide_place = lax.axis_index("wide")
    local_rows, sequences, model_width = tokens.shape
    block_rows = local_rows * narrow_count
    query_cols = w_query.shape[1]
    kv_cols = w_key.shape[1]
    kv_heads = kv_cols // HD
    heads = query_cols // HD
    group_size = heads // kv_heads
    score_scale = HD ** (-0.5)
    factor = rope_scale[0]
    token_count = local_rows * sequences

    token_float = tokens.swapaxes(0, 1).astype(jnp.float32)
    upstream_low = cotangent.swapaxes(0, 1)
    upstream = upstream_low.astype(jnp.float32)
    upstream_all = lax.all_gather(
        upstream_low.reshape(token_count, model_width), "wide", axis=0, tiled=True
    )

    attn_inverse = inverse_of(token_float)
    attn_low = (token_float * attn_inverse * gain_attn).astype(jnp.bfloat16)
    attn_block = gather_narrow(attn_low, 0)
    query_weight = w_query.reshape(model_width, kv_heads, group_size, HD).swapaxes(1, 2)
    joint_weight = jnp.concatenate(
        [query_weight.reshape(model_width, query_cols), w_key, w_value], axis=1
    )
    out_weight = w_out.reshape(kv_heads, group_size, HD, model_width).swapaxes(0, 1)
    out_weight = out_weight.reshape(query_cols, model_width)
    joint_proj = jnp.einsum(
        "std,dc->stc", attn_block, joint_weight, preferred_element_type=jnp.float32
    )
    cosine, sine = angles_of(wide_place * block_rows + lax.iota(jnp.int32, block_rows), factor)
    head_cosine, head_sine = cosine[None, :, None, :], sine[None, :, None, :]

    query_rot = rotate(
        joint_proj[..., :query_cols].reshape(sequences, block_rows, heads, HD),
        head_cosine,
        head_sine,
    ).astype(jnp.bfloat16)
    query_low = (query_rot * jnp.bfloat16(score_scale)).reshape(sequences, block_rows, query_cols)
    key_rot = rotate(
        joint_proj[..., query_cols : query_cols + kv_cols].reshape(
            sequences, block_rows, kv_heads, HD
        ),
        head_cosine,
        head_sine,
    )
    key_local = key_rot.astype(jnp.bfloat16).reshape(sequences, block_rows, kv_cols)
    value_local = joint_proj[..., query_cols + kv_cols :].astype(jnp.bfloat16)
    pair_all, attn_result, out_low, log_total = attn_fwd(
        query_low, jnp.concatenate([key_local, value_local], axis=-1), 1
    )
    attn_branch = scatter_narrow(
        jnp.einsum("stc,cd->std", out_low, out_weight, preferred_element_type=jnp.float32).astype(
            jnp.bfloat16
        ),
        2,
    )
    residual = token_float + attn_branch
    moe_inverse = inverse_of(residual)
    moe_low = (residual * moe_inverse * gain_moe).astype(jnp.bfloat16)
    moe_flat = moe_low.reshape(token_count, model_width)

    expert_count = w_router.shape[1]
    local_experts = w_gate.shape[0]
    first_expert = wide_place * local_experts
    expert_ids = routes.swapaxes(0, 1).reshape(token_count, -1)
    onehot = expert_ids[:, :, None] == lax.iota(jnp.int32, expert_count)[None, None, :]
    named = jnp.sum(onehot.astype(jnp.float32), axis=1)
    logits = jnp.dot(moe_flat, w_router, preferred_element_type=jnp.float32)
    masked = jnp.where(named > 0, logits, MASKED)
    powers = jnp.exp(masked - jnp.max(masked, axis=-1, keepdims=True)) * named
    shares = powers / jnp.sum(powers, axis=-1, keepdims=True)

    moe_all, shares_all = gather_wide([moe_flat, shares.T[None]], (0, 0), True, 3)
    own_shares = lax.dynamic_slice_in_dim(shares_all, first_expert, local_experts, 1)
    own_shares = jnp.pad(own_shares, ((0, 0), (0, 8 - local_experts), (0, 0)))
    part_out, part_copy, own_picks, hidden_shared, signals = experts_both(
        moe_all, upstream_all, own_shares, w_gate, w_up, w_down
    )
    part_picks = lax.dynamic_update_slice_in_dim(
        jnp.zeros_like(shares_all), own_picks[:, :local_experts], first_expert, 1
    )

    def by_block(rows):
        return rows.reshape((wide_count, rows.shape[0] // wide_count) + rows.shape[1:])

    copy_sum, picks = scatter_wide([by_block(part_copy), part_picks], True, 4)
    moe_part = lax.psum_scatter(part_out, "wide", scatter_dimension=0, tiled=True).astype(
        jnp.float32
    )
    layer_out = (residual + moe_part.reshape(residual.shape)).astype(jnp.bfloat16)

    width = w_gate.shape[2]
    expert_grads = tuple(
        lax.psum_scatter(update, "narrow", scatter_dimension=1, tiled=True).astype(jnp.float32)
        for update in (
            *turned_product(moe_all, signals, block_rows // 2, 2, local_experts),
            turned_product(hidden_shared, upstream_all, block_rows // 2, 1, 1)[0].reshape(
                local_experts, width, model_width
            ),
        )
    )

    picks = picks.T
    logit_grads = shares * (picks - jnp.sum(shares * picks, axis=-1, keepdims=True))
    router_grads = jnp.dot(logit_grads.T, moe_flat.astype(jnp.float32), precision=PRECISE)
    moe_grads = jnp.dot(logit_grads, w_router.astype(jnp.float32).T, precision=PRECISE)
    moe_grads = moe_grads + copy_sum
    norm_grads, moe_gain = normalize_back(
        residual, moe_inverse, gain_moe, moe_grads.reshape(residual.shape)
    )
    residual_grads = upstream + norm_grads
    branch_all = gather_narrow(residual_grads.astype(jnp.bfloat16), 6)
    attended_grads = jnp.einsum(
        "std,cd->stc", branch_all, out_weight, preferred_element_type=jnp.float32
    ).astype(jnp.bfloat16)
    query_grads, pair_own = attn_bwd(
        score_scale, query_low, attended_grads, attn_result, log_total, pair_all, 7
    )
    out_update = jnp.einsum("stc,std->cd", out_low, branch_all, preferred_element_type=jnp.float32)
    query_turned = rotate(
        query_grads.reshape(sequences, block_rows, heads, HD), head_cosine, -head_sine
    ).astype(jnp.bfloat16)
    key_low = rotate(
        pair_own[..., :kv_cols].reshape(sequences, block_rows, kv_heads, HD),
        head_cosine,
        -head_sine,
    ).astype(jnp.bfloat16)
    joint_grads = jnp.concatenate(
        [
            query_turned.reshape(sequences, block_rows, query_cols),
            key_low.reshape(sequences, block_rows, kv_cols),
            pair_own[..., kv_cols:].astype(jnp.bfloat16),
        ],
        axis=-1,
    )
    joint_update = jnp.einsum(
        "std,stc->dc", attn_block, joint_grads, preferred_element_type=jnp.float32
    )
    attn_grads = scatter_narrow(
        jnp.einsum(
            "stc,dc->std", joint_grads, joint_weight, preferred_element_type=jnp.float32
        ).astype(jnp.bfloat16),
        8,
    )
    token_grads, attn_gain = normalize_back(token_float, attn_inverse, gain_attn, attn_grads)
    token_grads = residual_grads + token_grads
    weight_updates = jnp.concatenate([joint_update, out_update.T], axis=1).astype(jnp.bfloat16)
    (joint_summed,) = scatter_wide([by_block(weight_updates)], True, 9)
    out_summed = joint_summed[:, query_cols + 2 * kv_cols :]
    small_parts = jnp.concatenate([router_grads, moe_gain[None, :], attn_gain[None, :]], axis=0)
    small_parts = jnp.pad(small_parts, ((0, -small_parts.shape[0] % 8), (0, 0)))
    small_summed = small_sum(small_parts, 10)
    return (
        layer_out.swapaxes(0, 1),
        token_grads.swapaxes(0, 1),
        small_summed[expert_count + 1],
        joint_summed[:, :query_cols]
        .reshape(-1, group_size, kv_heads, HD)
        .swapaxes(1, 2)
        .reshape(-1, query_cols),
        joint_summed[:, query_cols : query_cols + kv_cols],
        joint_summed[:, query_cols + kv_cols : query_cols + 2 * kv_cols],
        out_summed.T.reshape(group_size, kv_heads, HD, -1).swapaxes(0, 1).reshape(query_cols, -1),
        small_summed[expert_count],
        small_summed[:expert_count].T,
        expert_grads[0],
        expert_grads[1],
        expert_grads[2],
    )


def solution(mesh):
    return jax.shard_map(
        on_device,
        mesh=mesh,
        in_specs=(
            P(("wide", "narrow"), None, None),
            P(),
            P(None, "narrow"),
            P(None, "narrow"),
            P(None, "narrow"),
            P("narrow", None),
            P(),
            P(),
            P("wide", None, None),
            P("wide", None, None),
            P("wide", None, None),
            P(("wide", "narrow"), None, None),
            P(),
            P(("wide", "narrow"), None, None),
        ),
        out_specs=(
            P(("wide", "narrow"), None, None),
            P(("wide", "narrow"), None, None),
            P(),
            P("wide", "narrow"),
            P("wide", "narrow"),
            P("wide", "narrow"),
            P("narrow", "wide"),
            P(),
            P(),
            P("wide", "narrow", None),
            P("wide", "narrow", None),
            P("wide", "narrow", None),
        ),
        check_vma=False,
    )
```
